256 devices in a mesh: wide: 16 (over x, y_lo, core), narrow: 16 (over y_hi, z).
Axes of the slice: x: 4, y: 4 (y_hi: 2, y_lo: 2; y = y_hi * 2 + y_lo), z: 8, core: 2. Of those that a mesh axis runs over, the one named last changes fastest.
Arguments:
- pose_feats: bfloat16 [16384, 1024], P(('wide', 'narrow')), may hold values from -3 to 3
- text_feats: bfloat16 [16384, 1024], P(('wide', 'narrow')), may hold values from -3 to 3
- match: int32 [16384], P(('wide', 'narrow')), may hold values from 0 to 16383, as said below
- pose_head: bfloat16 [1024, 1024], replicated, may hold values from -1 to 1
- text_head: bfloat16 [1024, 1024], replicated, may hold values from -1 to 1
Outputs:
- loss: float32 [], replicated
- grad_pose: float32 [16384, 1024], P(('wide', 'narrow'))
- grad_text: float32 [16384, 1024], P(('wide', 'narrow'))
- head_grads: float32 [1024, 2048], P('wide')
The draws below stay inside these ranges and needn't reach their ends.
Inputs may be any that keep to these rules, and one draw needn't show every extreme that they name: `match`: every text index appears exactly once.
All inputs are finite; a program needn't handle non-finite values.
Results may differ from the reference program's by a relative error of at most 0.0049.
Values may be sent and summed in bfloat16 or wider, within the bound.
No kernel may reach another device: no remote copies, remote signals or barrier semaphores. Data moves between devices by JAX's collectives and lax.ppermute only.
A program may use at most 64 MiB of HBM per device.

```python
import math
import jax
import jax.numpy as jnp
from jax import lax

D = 1024
E = 1024
GROUP = 1024
BATCH = 16384


def common_direction(key):
    return jnp.clip(jax.random.normal(jax.random.fold_in(key, 3), (D,), jnp.float32), -3.0, 3.0)


def paired_order(key):
    return jax.random.permutation(jax.random.fold_in(key, 4), BATCH).astype(jnp.int32)


def pose_noise(key):
    gauss = jax.random.normal(jax.random.fold_in(key, 5), (BATCH, D), jnp.float32)
    return gauss


def shared_head(key):
    return jnp.clip(jax.random.normal(jax.random.fold_in(key, 9), (D, E), jnp.float32), -4.0, 4.0) / math.sqrt(D)


def feature_rows(key, direction, lift_rows, noise_part):
    row_scale = jnp.exp(jax.random.uniform(key, (BATCH, 1), jnp.float32, math.log(0.3), math.log(3.0)))
    rows = row_scale * (noise_part + lift_rows[:, None] * direction[None, :]) / math.sqrt(D)
    return jnp.clip(rows, -3.0, 3.0).astype(jnp.bfloat16)


def draw_pose_feats(key, part):
    direction = common_direction(key)
    gauss = pose_noise(key)
    key = jax.random.fold_in(key, 11)
    position = jnp.arange(BATCH, dtype=jnp.float32) / BATCH
    noise_part = jnp.clip(gauss, -4.0, 4.0)
    lift_rows = 0.1 + 0.9 * position
    return feature_rows(key, direction, lift_rows, noise_part)


def draw_text_feats(key, part):
    direction = common_direction(key)
    gauss = pose_noise(key)
    source = jnp.argsort(paired_order(key)).astype(jnp.int32)
    key = jax.random.fold_in(key, 23)
    own_key, share_key, scale_key = jax.random.split(key, 3)
    share = jax.random.uniform(share_key, (BATCH, 1), jnp.float32, 0.05, 0.35)
    paired = jnp.clip(gauss[source], -4.0, 4.0)
    own = jnp.clip(jax.random.normal(own_key, (BATCH, D), jnp.float32), -4.0, 4.0)
    lift_rows = jnp.full((BATCH,), 0.05, jnp.float32)
    noise_part = share * paired + jnp.sqrt(1.0 - share * share) * own
    return feature_rows(scale_key, direction, lift_rows, noise_part)


def draw_match(key, part):
    return paired_order(key)


def draw_pose_head(key, part):
    return shared_head(key).astype(jnp.bfloat16)


def draw_text_head(key, part):
    base = shared_head(key)
    key = jax.random.fold_in(key, 31)
    other = jnp.clip(jax.random.normal(key, (D, E), jnp.float32), -4.0, 4.0) / math.sqrt(D)
    return (0.9 * base + math.sqrt(0.19) * other).astype(jnp.bfloat16)


def setup_inputs(seed: int = 0) -> dict:
    arg_keys = jax.random.split(jax.random.key(seed), 6)
    pose_feats = draw_pose_feats(jax.random.fold_in(arg_keys[5], 71), 0)
    text_feats = draw_text_feats(jax.random.fold_in(arg_keys[5], 71), 0)
    match = draw_match(jax.random.fold_in(arg_keys[5], 71), 0)
    pose_head = draw_pose_head(jax.random.fold_in(arg_keys[5], 71), 0)
    text_head = draw_text_head(jax.random.fold_in(arg_keys[5], 71), 0)
    return dict(pose_feats=pose_feats, text_feats=text_feats, match=match, pose_head=pose_head, text_head=text_head)


epsilon = 1e-06
logit_bias = -10.0

def unit_rows(raw_rows):
    norm_rows = jnp.sqrt(lax.optimization_barrier(jnp.sum(raw_rows * raw_rows, axis=1, keepdims=True)) + epsilon)
    return (raw_rows / norm_rows, norm_rows)

def back_rows(grad_rows, unit_vals, norm_rows):
    inner_part = lax.optimization_barrier(jnp.sum(unit_vals * grad_rows, axis=1, keepdims=True))
    return ((grad_rows - unit_vals * inner_part) / norm_rows).astype(jnp.bfloat16)

def reference(pose_feats, text_feats, match, pose_head, text_head):
    pose_unit, pose_norm = unit_rows(jnp.dot(pose_feats, pose_head, preferred_element_type=jnp.float32))
    text_unit, text_norm = unit_rows(jnp.dot(text_feats, text_head, preferred_element_type=jnp.float32))
    pose_embed = pose_unit.astype(jnp.bfloat16)
    text_embed = text_unit.astype(jnp.bfloat16)
    logit_scale = 2.0 * math.sqrt(E)
    grad_scale = logit_scale / math.sqrt(BATCH)
    block_count = BATCH // GROUP
    text_ids = jnp.arange(BATCH, dtype=jnp.int32)

    def visit(carry, inputs):
        loss_total, pose_grad = carry
        text_block, block_ids = inputs
        logits = logit_scale * lax.dot_general(text_block, pose_embed, (((1,), (1,)), ((), ())), preferred_element_type=jnp.float32) + logit_bias
        pair_sign = jnp.where(match[None, :] == block_ids[:, None], 1.0, -1.0).astype(jnp.float32)
        loss_total = loss_total + jnp.sum(jax.nn.softplus(-pair_sign * logits))
        weights = (-pair_sign * jax.nn.sigmoid(-pair_sign * logits) * grad_scale).astype(jnp.bfloat16)
        pose_grad = pose_grad + lax.dot_general(weights, text_block, (((0,), (0,)), ((), ())), preferred_element_type=jnp.float32)
        text_part = jnp.dot(weights, pose_embed, preferred_element_type=jnp.float32)
        return ((loss_total, pose_grad), text_part)
    start_state = (jnp.zeros((), jnp.float32), jnp.zeros((BATCH, E), jnp.float32))
    (loss_total, pose_grad), text_parts = lax.scan(visit, start_state, (text_embed.reshape(block_count, GROUP, E), text_ids.reshape(block_count, GROUP)))
    text_grad = text_parts.reshape(BATCH, E)
    pose_back = back_rows(pose_grad, pose_unit, pose_norm)
    text_back = back_rows(text_grad, text_unit, text_norm)
    grad_pose = jnp.dot(pose_back, pose_head.T, preferred_element_type=jnp.float32)
    grad_text = jnp.dot(text_back, text_head.T, preferred_element_type=jnp.float32)
    head_grads = jnp.concatenate([jnp.dot(pose_feats.T, pose_back, preferred_element_type=jnp.float32), jnp.dot(text_feats.T, text_back, preferred_element_type=jnp.float32)], axis=1)
    loss = loss_total / (BATCH * BATCH)
    return (loss, grad_pose, grad_text, head_grads)
```

```python
import functools
import math

import jax
import jax.numpy as jnp
from jax import lax
from jax.experimental import pallas as pl
from jax.experimental.pallas import tpu as pltpu
from jax.sharding import Mesh
from jax.sharding import PartitionSpec as P

epsilon = 1e-06
logit_bias = -10.0

AXES = ("x", "yl", "core", "yh", "z")
PLANE = ("x", "yl", "yh")
LINE = ("core", "z")
NARROW = ("yh", "z")
NX, NY, NZ, NC = 4, 4, 8, 2
ROWS = 64
N = 1024
EXTRA = 128
TILE = 256

NT = (((1,), (1,)), ((), ()))
TN = (((0,), (0,)), ((), ()))
NN = (((1,), (0,)), ((), ()))


def device_index(x, y, z, c):
    return (((x * 2 + y % 2) * 2 + c) * 2 + y // 2) * NZ + z


def pairs_of(move):
    out = []
    for x in range(NX):
        for y in range(NY):
            for z in range(NZ):
                for c in range(NC):
                    x2, y2, z2, c2 = move(x, y, z, c)
                    out.append(
                        (device_index(x, y, z, c), device_index(x2 % NX, y2 % NY, z2 % NZ, c2 % NC))
                    )
    return out


def send(value, move):
    return lax.ppermute(value, AXES, pairs_of(move))


def swap_cores(value):
    return send(value, lambda x, y, z, c: (x, y, z, 1 - c))


def plane_step(first, by):
    def move(x, y, z, c):
        return (x + by, y, z, c) if (c == 0) == first else (x, y + by, z, c)

    return move


def ring_gather(shard, first, place):
    half = shard.shape[0] // 2
    below = send(shard, plane_step(first, 1))
    above = send(shard, plane_step(first, -1))
    far_low = send(below[:half], plane_step(first, 1))
    far_high = send(above[half:], plane_step(first, -1))
    rows = shard.shape[0]
    out = jnp.zeros((4 * rows, shard.shape[1]), shard.dtype)
    for value, offset, start in (
        (shard, 0, 0),
        (below, 3, 0),
        (above, 1, 0),
        (far_low, 2, 0),
        (far_high, 2, half),
    ):
        out = lax.dynamic_update_slice(out, value, ((place + offset) % 4 * rows + start, 0))
    return out


def project_kernel(feats_ref, head_ref, embed_ref, unit_ref, norm_ref):
    @pl.loop(0, N // TILE)
    def _(step):
        cols = pl.ds(pl.multiple_of(step * TILE, TILE), TILE)
        raw = lax.dot_general(
            head_ref[...], feats_ref[cols, :N], NT, preferred_element_type=jnp.float32
        )
        norm = jnp.sqrt(jnp.sum(raw * raw, axis=0, keepdims=True) + epsilon)
        unit = raw / norm
        unit_ref[:, cols] = unit
        embed_ref[:, cols] = unit.astype(jnp.bfloat16)
        norm_ref[:, cols] = jnp.broadcast_to(norm, (8, TILE))


def back_cols(grad, unit, norm):
    inner = jnp.sum(unit * grad, axis=0, keepdims=True)
    return ((grad - unit * inner) / norm).astype(jnp.bfloat16)


def pair_kernel(
    scale,
    grad_scale,
    feats_ref,
    head_ref,
    pose_ref,
    pose_unit_ref,
    pose_norm_ref,
    target_ref,
    loss_ref,
    pose_back_ref,
    text_back_ref,
    text_ref,
    weights_ref,
):
    loss_ref[...] = jnp.zeros_like(loss_ref)
    target = target_ref[0:1, :]

    @pl.loop(0, N // TILE)
    def _(step):
        start = pl.multiple_of(step * TILE, TILE)
        cols = pl.ds(start, TILE)
        raw = lax.dot_general(
            head_ref[...], feats_ref[cols, :], NT, preferred_element_type=jnp.float32
        )
        norm = jnp.sqrt(jnp.sum(raw * raw, axis=0, keepdims=True) + epsilon)
        unit = raw / norm
        text = unit.astype(jnp.bfloat16)
        text_ref[:, cols] = text
        logits = (
            scale * lax.dot_general(text, pose_ref[...], TN, preferred_element_type=jnp.float32)
            + logit_bias
        )
        ids = lax.broadcasted_iota(jnp.int32, (TILE, 1), 0) + start
        paired = ids == target
        arg = jnp.where(paired, -logits, logits)
        small = jnp.exp(-jnp.abs(arg))
        loss = jnp.maximum(arg, 0.0) + jnp.log1p(small)
        loss_ref[...] += jnp.sum(loss.reshape(TILE // 8, 8, N), axis=0)
        share = 1.0 / (1.0 + small)
        sig = jnp.where(arg >= 0.0, share, small * share)
        weights = (jnp.where(paired, -grad_scale, grad_scale) * sig).astype(jnp.bfloat16)
        weights_ref[cols, :] = weights
        text_grad = lax.dot_general(
            pose_ref[...], weights, NT, preferred_element_type=jnp.float32
        )
        text_back_ref[:, cols] = back_cols(text_grad, unit, norm)

    @pl.loop(0, N // TILE)
    def _(step):
        cols = pl.ds(pl.multiple_of(step * TILE, TILE), TILE)
        pose_grad = lax.dot_general(
            text_ref[...], weights_ref[:, cols], NN, preferred_element_type=jnp.float32
        )
        pose_back_ref[:, cols] = back_cols(
            pose_grad, pose_unit_ref[:, cols], pose_norm_ref[0:1, cols]
        )


VMEM = pl.BlockSpec(memory_space=pltpu.VMEM)
LIMIT = pltpu.CompilerParams(vmem_limit_bytes=48 * 1024 * 1024)


def project(feats, head_t):
    return pl.pallas_call(
        project_kernel,
        out_shape=(
            jax.ShapeDtypeStruct((N, N), jnp.bfloat16),
            jax.ShapeDtypeStruct((N, N), jnp.float32),
            jax.ShapeDtypeStruct((8, N), jnp.float32),
        ),
        in_specs=[VMEM] * 2,
        out_specs=(VMEM,) * 3,
        compiler_params=LIMIT,
        cost_estimate=pl.CostEstimate(flops=2 * N**3, bytes_accessed=12 * N * N, transcendentals=0),
    )(feats, head_t)


def score(scale, grad_scale, feats, head_t, pose, pose_unit, pose_norm, target):
    return pl.pallas_call(
        functools.partial(pair_kernel, scale, grad_scale),
        out_shape=(
            jax.ShapeDtypeStruct((8, N), jnp.float32),
            jax.ShapeDtypeStruct((N, N), jnp.bfloat16),
            jax.ShapeDtypeStruct((N, N), jnp.bfloat16),
        ),
        in_specs=[VMEM] * 6,
        out_specs=(VMEM,) * 3,
        scratch_shapes=[pltpu.VMEM((N, N), jnp.bfloat16), pltpu.VMEM((N, N), jnp.bfloat16)],
        compiler_params=LIMIT,
        cost_estimate=pl.CostEstimate(
            flops=8 * N**3, bytes_accessed=14 * N * N, transcendentals=3 * N * N
        ),
    )(feats, head_t, pose, pose_unit, pose_norm, target)


def local(pose_feats, text_feats, match, pose_head, text_head):
    batch_size = ROWS * 256
    logit_scale = 2.0 * math.sqrt(N)
    grad_scale = logit_scale / math.sqrt(batch_size)
    x = lax.axis_index("x")
    yl = lax.axis_index("yl")
    yh = lax.axis_index("yh")
    core = lax.axis_index("core")
    y = yh * 2 + yl
    first = core == 0

    text_group = lax.all_gather(text_feats, LINE, axis=0, tiled=True)
    ids = jnp.stack([match // 128, match % 128], axis=1).astype(jnp.bfloat16)
    shard = jnp.concatenate([pose_feats, jnp.pad(ids, ((0, 0), (0, EXTRA - 2)))], axis=1)
    pose_group = ring_gather(
        ring_gather(shard, True, jnp.where(first, x, y)), False, jnp.where(first, y, x)
    )
    pose_head_t = pose_head.T
    text_head_t = text_head.T

    pose, pose_unit, pose_norm = project(pose_group, pose_head_t)
    lanes = lax.broadcasted_iota(jnp.int32, (8, EXTRA), 1)
    pick = jnp.where(lanes == 0, 128.0, jnp.where(lanes == 1, 1.0, 0.0)).astype(jnp.bfloat16)
    group_ids = lax.dot_general(
        pick, pose_group[:, N:], NT, preferred_element_type=jnp.float32
    ).astype(jnp.int32)
    offset = group_ids - ((x * 2 + yl) * 2048 + yh * 512)
    inside = (offset >= 0) & (offset < 2048) & (offset % 1024 < 512)
    target = jnp.where(inside, offset // 1024 * 512 + offset % 1024, -1)

    loss_part, pose_part, text_part = score(
        logit_scale, grad_scale, text_group, text_head_t, pose, pose_unit, pose_norm, target
    )

    halves = text_part.reshape(2, N // 2, N)
    keep = lax.dynamic_index_in_dim(halves, core, 0, keepdims=False)
    give = lax.dynamic_index_in_dim(halves, 1 - core, 0, keepdims=False)
    got = swap_cores(give)
    text_sum = (keep.astype(jnp.float32) + got.astype(jnp.float32)).astype(jnp.bfloat16)
    text_back = lax.psum_scatter(text_sum, "z", scatter_dimension=0, tiled=True)

    parts = lax.all_to_all(pose_part.reshape(16, ROWS, N), PLANE, 0, 0)
    pose_back = jnp.sum(parts.astype(jnp.float32), axis=0).astype(jnp.bfloat16)

    pose_term = jnp.dot(pose_back, pose_group[:, :N], preferred_element_type=jnp.float32)
    text_term = jnp.dot(text_back, text_group, preferred_element_type=jnp.float32)

    pose_blocks = pose_term.reshape(ROWS, 8, 2, ROWS).transpose(2, 1, 0, 3).reshape(16, ROWS, ROWS)
    text_rows = text_back.astype(jnp.float32).reshape(ROWS, 16, ROWS).transpose(1, 0, 2)
    loss_rows = jnp.zeros((16, 8, 2 * ROWS), jnp.float32) + jnp.sum(loss_part)
    line = lax.all_to_all(
        jnp.concatenate([jnp.concatenate([pose_blocks, text_rows], axis=2), loss_rows], axis=1),
        LINE,
        0,
        0,
    )
    pose_sum = jnp.sum(line[:, :ROWS, :ROWS], axis=0)
    text_cols = line[:, :ROWS, ROWS:].reshape(N, ROWS).astype(jnp.bfloat16)
    loss_line = jnp.sum(line[:, ROWS, 0])

    text_blocks = text_term.reshape(ROWS, 16, ROWS).transpose(1, 0, 2)
    by_slot = pose_back.astype(jnp.float32).reshape(ROWS, 4, 4, ROWS)
    by_xy = jnp.where(first, by_slot.transpose(2, 1, 0, 3), by_slot.transpose(1, 2, 0, 3))
    pose_rows = (
        by_xy.reshape(4, 2, 2, ROWS, ROWS).transpose(0, 2, 1, 3, 4).reshape(16, ROWS, ROWS)
    )
    loss_rows = jnp.zeros((16, 8, 2 * ROWS), jnp.float32) + loss_line
    plane = lax.all_to_all(
        jnp.concatenate([jnp.concatenate([text_blocks, pose_rows], axis=2), loss_rows], axis=1),
        PLANE,
        0,
        0,
    )
    text_sum = jnp.sum(plane[:, :ROWS, :ROWS], axis=0)
    pose_cols = plane[:, :ROWS, ROWS:].reshape(N, ROWS).astype(jnp.bfloat16)
    loss = jnp.sum(plane[:, ROWS, 0]) / (batch_size * batch_size)

    grad_text = lax.dot_general(text_cols, text_head_t, TN, preferred_element_type=jnp.float32)
    grad_pose = lax.dot_general(pose_cols, pose_head_t, TN, preferred_element_type=jnp.float32)

    pose_mine = send(
        pose_sum.T, lambda x, y, z, c: (z // 2, y // 2 * 2 + z % 2, x * 2 + y % 2, c)
    )
    text_mine = send(text_sum.T, lambda x, y, z, c: (x, c * 2 + y % 2, z, y // 2))
    mine = jnp.concatenate([pose_mine, text_mine], axis=1)
    every = lax.all_to_all(jnp.broadcast_to(mine[None], (16, ROWS, 2 * ROWS)), NARROW, 0, 0)
    pose_cat = (
        every[:, :, :ROWS].reshape(2, 8, ROWS, ROWS).transpose(2, 1, 0, 3).reshape(ROWS, N)
    )
    text_cat = every[:, :, ROWS:].transpose(1, 0, 2).reshape(ROWS, N)
    return (loss, grad_pose, grad_text, jnp.concatenate([pose_cat, text_cat], axis=1))


def solution(mesh):
    fine = Mesh(mesh.devices.reshape(NX, 2, NC, 2, NZ), AXES)
    placed = (P(AXES, None), P(AXES, None), P(AXES), P(), P())
    return jax.shard_map(
        local,
        mesh=fine,
        in_specs=placed,
        out_specs=(P(), P(AXES, None), P(AXES, None), P(("x", "yl", "core"), None)),
        check_vma=False,
    )
```

```python
import functools
import math

import jax
import jax.numpy as jnp
from jax import lax
from jax.experimental import pallas as pl
from jax.experimental.pallas import tpu as pltpu
from jax.sharding import Mesh
from jax.sharding import PartitionSpec as P

epsilon = 1e-06
logit_bias = -10.0
log1p_terms = (
    0.9999999403953552,
    -0.4999944567680359,
    0.3331812024116516,
    -0.2483539879322052,
    0.19076880812644958,
    -0.13602247834205627,
    0.0775160863995552,
    -0.029074065387248993,
    0.005126102361828089,
)

AXES = ("x", "yl", "core", "yh", "z")
PLANE = ("x", "yl", "yh")
LINE = ("core", "z")
NARROW = ("yh", "z")
NX, NY, NZ, NC = 4, 4, 8, 2
ROWS = 64
N = 1024
EXTRA = 128
TILE = 512
STEPS = N // TILE

NT = (((1,), (1,)), ((), ()))
TN = (((0,), (0,)), ((), ()))
NN = (((1,), (0,)), ((), ()))


def device_index(x, y, z, c):
    return (((x * 2 + y % 2) * 2 + c) * 2 + y // 2) * NZ + z


def pairs_of(move):
    out = []
    for x in range(NX):
        for y in range(NY):
            for z in range(NZ):
                for c in range(NC):
                    x2, y2, z2, c2 = move(x, y, z, c)
                    out.append(
                        (device_index(x, y, z, c), device_index(x2 % NX, y2 % NY, z2 % NZ, c2 % NC))
                    )
    return out


def send(value, move):
    return lax.ppermute(value, AXES, pairs_of(move))


def swap_cores(value):
    return send(value, lambda x, y, z, c: (x, y, z, 1 - c))


def plane_groups(x_core):
    groups = []
    for c in range(NC):
        for z in range(NZ):
            if c == x_core:
                groups += [[device_index(x, y, z, c) for x in range(NX)] for y in range(NY)]
            else:
                groups += [[device_index(x, y, z, c) for y in (0, 2, 1, 3)] for x in range(NX)]
    return groups


def ring_gather(shard, move, place, slot):
    rows = shard.shape[0]
    half = rows // 2
    below = send(shard, move(1))
    above = send(shard, move(-1))
    far_low = send(below[:half], move(1))
    far_high = send(above[half:], move(-1))
    out = jnp.zeros((4 * rows, shard.shape[1]), shard.dtype)
    for value, offset, start in (
        (shard, 0, 0),
        (below, 3, 0),
        (above, 1, 0),
        (far_low, 2, 0),
        (far_high, 2, half),
    ):
        at = slot((place + offset) % 4) * rows + start
        out = lax.dynamic_update_slice(out, value, (at, 0))
    return out


def along_x(by):
    return lambda x, y, z, c: (x + by, y, z, c)


def along_y(by):
    return lambda x, y, z, c: (x, y + by, z, c)


def dot(a, b, dims):
    return lax.dot_general(a, b, dims, preferred_element_type=jnp.float32)


def inverse_norm(raw):
    return lax.rsqrt(jnp.sum(raw * raw, axis=0, keepdims=True) + epsilon)


def reciprocal(value):
    guess = pltpu.reciprocal(value, approx=True)
    return guess * (2.0 - value * guess)


def back_cols(grad, unit, inverse):
    inner = jnp.sum(unit * grad, axis=0, keepdims=True)
    return ((grad - unit * inner) * inverse).astype(jnp.bfloat16)


def cols(step):
    return slice(step * TILE, (step + 1) * TILE)


def project_kernel(feats_ref, head_ref, embed_ref, unit_ref, inverse_ref):
    raw = [dot(head_ref[...], feats_ref[cols(0), :N], NT)]
    for step in range(STEPS):
        if step + 1 < STEPS:
            raw.append(dot(head_ref[...], feats_ref[cols(step + 1), :N], NT))
        inverse = inverse_norm(raw[step])
        unit = raw[step] * inverse
        unit_ref[:, cols(step)] = unit
        embed_ref[:, cols(step)] = unit.astype(jnp.bfloat16)
        inverse_ref[:, cols(step)] = jnp.broadcast_to(inverse, (8, TILE))


def pair_kernel(
    scale,
    grad_scale,
    feats_hbm,
    head_hbm,
    pose_hbm,
    pose_unit_hbm,
    pose_inverse_ref,
    target_ref,
    loss_ref,
    text_inverse_ref,
    pose_back_hbm,
    weights_hbm,
    text_unit_hbm,
    feats_ref,
    head_ref,
    pose_ref,
    pose_unit_ref,
    text_ref,
    weights_ref,
    text_unit_ref,
    pose_back_ref,
    in_sems,
    out_sems,
):
    head_in = pltpu.make_async_copy(head_hbm, head_ref, in_sems.at[0])
    feats_in = [
        pltpu.make_async_copy(feats_hbm.at[cols(s), :], feats_ref.at[cols(s), :], in_sems.at[1 + s])
        for s in range(STEPS)
    ]
    pose_in = pltpu.make_async_copy(pose_hbm, pose_ref, in_sems.at[1 + STEPS])
    unit_in = pltpu.make_async_copy(pose_unit_hbm, pose_unit_ref, in_sems.at[2 + STEPS])
    for copy in (head_in, *feats_in, pose_in, unit_in):
        copy.start()

    raws = []
    head_in.wait()
    for step in range(STEPS):
        feats_in[step].wait()
        raws.append(dot(head_ref[...], feats_ref[cols(step), :], NT))
    out = []
    for step in range(STEPS):
        inverse = inverse_norm(raws[step])
        unit = raws[step] * inverse
        text_inverse_ref[:, cols(step)] = jnp.broadcast_to(inverse, (8, TILE))
        text_unit_ref[:, cols(step)] = unit
        text_ref[:, cols(step)] = unit.astype(jnp.bfloat16)
        copy = pltpu.make_async_copy(
            text_unit_ref.at[:, cols(step)], text_unit_hbm.at[:, cols(step)], out_sems.at[step]
        )
        copy.start()
        out.append(copy)

    pose_in.wait()
    target = target_ref[0:1, :]
    inner = [dot(text_ref[:, cols(0)], pose_ref[...], TN)]
    loss_sum = None
    for step in range(STEPS):
        if step + 1 < STEPS:
            inner.append(dot(text_ref[:, cols(step + 1)], pose_ref[...], TN))
        logits = scale * inner[step] + logit_bias
        ids = lax.broadcasted_iota(jnp.int32, (TILE, 1), 0) + step * TILE
        paired = ids == target
        arg = jnp.where(paired, -logits, logits)
        small = jnp.exp(-jnp.abs(arg))
        sig = jnp.where(arg >= 0.0, 1.0, small) * reciprocal(1.0 + small)
        weights_ref[cols(step), :] = (jnp.where(paired, -grad_scale, grad_scale) * sig).astype(
            jnp.bfloat16
        )
        copy = pltpu.make_async_copy(
            weights_ref.at[cols(step), :], weights_hbm.at[cols(step), :], out_sems.at[STEPS + step]
        )
        copy.start()
        out.append(copy)
        poly = jnp.full_like(small, log1p_terms[-1])
        for term in log1p_terms[-2::-1]:
            poly = poly * small + term
        loss = jnp.maximum(arg, 0.0) + small * poly
        part = jnp.sum(loss.reshape(TILE // 8, 8, N), axis=0)
        loss_sum = part if loss_sum is None else loss_sum + part
    loss_ref[...] = loss_sum

    unit_in.wait()
    second = lax.axis_index("core")
    grads = [dot(text_ref[...], weights_ref[:, cols(0)], NN)]
    for step in range(STEPS):
        if step + 1 < STEPS:
            grads.append(dot(text_ref[...], weights_ref[:, cols(step + 1)], NN))
        pose_back_ref[:, cols(step)] = back_cols(
            grads[step], pose_unit_ref[:, cols(step)], pose_inverse_ref[0:1, cols(step)]
        )
        for block in range(16):
            to = block + second * (block % 4 * 4 + block // 4 - block)
            copy = pltpu.make_async_copy(
                pose_back_ref.at[block * ROWS : (block + 1) * ROWS, cols(step)],
                pose_back_hbm.at[pl.ds(pl.multiple_of(to * ROWS, ROWS), ROWS), cols(step)],
                out_sems.at[2 * STEPS + step * 16 + block],
            )
            copy.start()
            out.append(copy)
    for copy in out:
        copy.wait()


def text_kernel(
    pose_hbm,
    weights_hbm,
    unit_hbm,
    inverse_ref,
    back_hbm,
    pose_ref,
    weights_ref,
    unit_ref,
    back_ref,
    in_sems,
    out_sems,
):
    pose_in = pltpu.make_async_copy(pose_hbm, pose_ref, in_sems.at[0])
    pose_in.start()
    weights_in, unit_in = [], []
    for step in range(STEPS):
        weights_in.append(
            pltpu.make_async_copy(
                weights_hbm.at[cols(step), :], weights_ref.at[cols(step), :], in_sems.at[1 + step]
            )
        )
        weights_in[step].start()
    for step in range(STEPS):
        unit_in.append(
            pltpu.make_async_copy(
                unit_hbm.at[:, cols(step)], unit_ref.at[:, cols(step)], in_sems.at[1 + STEPS + step]
            )
        )
        unit_in[step].start()
    pose_in.wait()
    weights_in[0].wait()
    grads = [dot(pose_ref[...], weights_ref[cols(0), :], NT)]
    out = []
    for step in range(STEPS):
        if step + 1 < STEPS:
            weights_in[step + 1].wait()
            grads.append(dot(pose_ref[...], weights_ref[cols(step + 1), :], NT))
        unit_in[step].wait()
        back_ref[:, cols(step)] = back_cols(
            grads[step], unit_ref[:, cols(step)], inverse_ref[0:1, cols(step)]
        )
        copy = pltpu.make_async_copy(
            back_ref.at[:, cols(step)], back_hbm.at[:, cols(step)], out_sems.at[step]
        )
        copy.start()
        out.append(copy)
    for copy in out:
        copy.wait()


VMEM = pl.BlockSpec(memory_space=pltpu.VMEM)
ANY = pl.BlockSpec(memory_space=pl.ANY)
LIMIT = pltpu.CompilerParams(vmem_limit_bytes=48 * 1024 * 1024)


def shape(rows, dtype):
    return jax.ShapeDtypeStruct((rows, N), dtype)


def project(feats, head_t):
    return pl.pallas_call(
        project_kernel,
        out_shape=(shape(N, jnp.bfloat16), shape(N, jnp.float32), shape(8, jnp.float32)),
        in_specs=[VMEM] * 2,
        out_specs=(VMEM,) * 3,
        compiler_params=LIMIT,
        cost_estimate=pl.CostEstimate(flops=2 * N**3, bytes_accessed=12 * N * N, transcendentals=0),
    )(feats, head_t)


def score(scale, grad_scale, feats, head_t, pose, pose_unit, pose_inverse, target):
    half = pltpu.VMEM((N, N), jnp.bfloat16)
    full = pltpu.VMEM((N, N), jnp.float32)
    return pl.pallas_call(
        functools.partial(pair_kernel, scale, grad_scale),
        out_shape=(
            shape(8, jnp.float32),
            shape(8, jnp.float32),
            shape(N, jnp.bfloat16),
            shape(N, jnp.bfloat16),
            shape(N, jnp.float32),
        ),
        in_specs=[ANY] * 4 + [VMEM] * 2,
        out_specs=(VMEM, VMEM, ANY, ANY, ANY),
        scratch_shapes=[
            half,
            half,
            half,
            full,
            half,
            half,
            full,
            half,
            pltpu.SemaphoreType.DMA((3 + STEPS,)),
            pltpu.SemaphoreType.DMA((18 * STEPS,)),
        ],
        compiler_params=LIMIT,
        cost_estimate=pl.CostEstimate(
            flops=6 * N**3, bytes_accessed=18 * N * N, transcendentals=2 * N * N
        ),
    )(feats, head_t, pose, pose_unit, pose_inverse, target)


def text_grads(pose, weights, unit, inverse):
    half = pltpu.VMEM((N, N), jnp.bfloat16)
    full = pltpu.VMEM((N, N), jnp.float32)
    return pl.pallas_call(
        text_kernel,
        out_shape=shape(N, jnp.bfloat16),
        in_specs=[ANY] * 3 + [VMEM],
        out_specs=ANY,
        scratch_shapes=[
            half,
            half,
            full,
            half,
            pltpu.SemaphoreType.DMA((1 + 2 * STEPS,)),
            pltpu.SemaphoreType.DMA((STEPS,)),
        ],
        compiler_params=LIMIT,
        cost_estimate=pl.CostEstimate(flops=2 * N**3, bytes_accessed=10 * N * N, transcendentals=0),
    )(pose, weights, unit, inverse)


def three_parts(value):
    high = lax.reduce_precision(value, 8, 7)
    middle = lax.reduce_precision(value - high, 8, 7)
    low = value - high - middle
    rows = lax.broadcasted_iota(jnp.int32, (16, ROWS), 0)
    block = jnp.where(rows == 0, high, jnp.where(rows == 1, middle, jnp.where(rows == 2, low, 0.0)))
    return block.astype(jnp.bfloat16)


def sum_parts(blocks):
    return jnp.sum(blocks[:, ROWS : ROWS + 3, 0].astype(jnp.float32))


def with_loss(blocks, loss):
    parts = jnp.broadcast_to(three_parts(loss)[None], (blocks.shape[0], 16, ROWS))
    return jnp.concatenate([blocks.astype(jnp.bfloat16), parts], axis=1)


def local(pose_feats, text_feats, match, pose_head, text_head):
    batch_size = ROWS * 256
    logit_scale = 2.0 * math.sqrt(N)
    grad_scale = logit_scale / math.sqrt(batch_size)
    x = lax.axis_index("x")
    yl = lax.axis_index("yl")
    yh = lax.axis_index("yh")
    core = lax.axis_index("core")
    z = lax.axis_index("z")

    text_group = lax.all_gather(text_feats, LINE, axis=0, tiled=True)
    ids = jnp.stack([match // 128, match % 128], axis=1).astype(jnp.bfloat16)
    shard = jnp.concatenate([pose_feats, jnp.pad(ids, ((0, 0), (0, EXTRA - 2)))], axis=1)
    pose_group = ring_gather(shard, along_y, yh * 2 + yl, lambda y: y % 2 * 2 + y // 2)
    pose_group = ring_gather(pose_group, along_x, x, lambda x: x)
    pose_head_t = pose_head.T
    text_head_t = text_head.T

    pose, pose_unit, pose_inverse = project(pose_group, pose_head_t)
    lanes = lax.broadcasted_iota(jnp.int32, (8, EXTRA), 1)
    pick = jnp.where(lanes == 0, 128.0, jnp.where(lanes == 1, 1.0, 0.0)).astype(jnp.bfloat16)
    group_ids = dot(pick, pose_group[:, N:], NT).astype(jnp.int32)
    offset = group_ids - ((x * 2 + yl) * 2048 + yh * 512)
    inside = (offset >= 0) & (offset < 2048) & (offset % 1024 < 512)
    target = jnp.where(inside, offset // 1024 * 512 + offset % 1024, -1)

    loss_part, text_inverse, pose_part, weights, text_unit = score(
        logit_scale, grad_scale, text_group, text_head_t, pose, pose_unit, pose_inverse, target
    )
    parts = lax.all_to_all(
        pose_part.reshape(4, 4 * ROWS, N), AXES, 0, 0, axis_index_groups=plane_groups(0)
    )
    text_part = text_grads(pose, weights, text_unit, text_inverse)

    halves = text_part.reshape(2, N // 2, N)
    keep = lax.dynamic_index_in_dim(halves, core, 0, keepdims=False)
    give = lax.dynamic_index_in_dim(halves, 1 - core, 0, keepdims=False)
    got = swap_cores(give)
    text_half = (keep.astype(jnp.float32) + got.astype(jnp.float32)).astype(jnp.bfloat16)
    text_back = lax.psum_scatter(text_half, "z", scatter_dimension=0, tiled=True)

    pose_sum = jnp.sum(parts.astype(jnp.float32), axis=0).astype(jnp.bfloat16)
    parts = lax.all_to_all(
        pose_sum.reshape(4, ROWS, N), AXES, 0, 0, axis_index_groups=plane_groups(1)
    )
    pose_back = jnp.sum(parts.astype(jnp.float32), axis=0).astype(jnp.bfloat16)

    pose_term = jnp.dot(pose_back, pose_group[:, :N], preferred_element_type=jnp.float32)
    pose_blocks = pose_term.reshape(ROWS, 8, 2, ROWS).transpose(2, 1, 0, 3).reshape(16, ROWS, ROWS)
    line = lax.all_to_all(with_loss(pose_blocks, jnp.sum(loss_part)), LINE, 0, 0)
    pose_sum = jnp.sum(line[:, :ROWS].astype(jnp.float32), axis=0)
    loss_line = sum_parts(line)
    pose_mine = send(
        with_loss(pose_sum.T[None], loss_line)[0],
        lambda x, y, z, c: (z // 2, y // 2 * 2 + z % 2, x * 2 + y % 2, c),
    )

    text_rows = lax.all_gather(text_back, LINE, axis=0, tiled=True)
    text_term = jnp.dot(text_back, text_group, preferred_element_type=jnp.float32)
    text_blocks = text_term.astype(jnp.bfloat16).reshape(ROWS, 16, ROWS).transpose(1, 0, 2)
    pose_rows = pose_back.reshape(ROWS, 16, ROWS).transpose(1, 0, 2)
    plane = lax.all_to_all(jnp.concatenate([text_blocks, pose_rows], axis=2), PLANE, 0, 0)
    text_sum = jnp.sum(plane[:, :, :ROWS].astype(jnp.float32), axis=0)
    text_mine = send(
        text_sum.T.astype(jnp.bfloat16), lambda x, y, z, c: (x, c * 2 + y % 2, z, y // 2)
    )

    mine = jnp.concatenate([pose_mine, jnp.pad(text_mine, ((0, 16), (0, 0)))], axis=1)
    every = lax.all_to_all(jnp.broadcast_to(mine[None], (16, ROWS + 16, 2 * ROWS)), NARROW, 0, 0)
    loss = sum_parts(every) / (batch_size * batch_size)
    pose_cat = (
        every[:, :ROWS, :ROWS].reshape(2, 8, ROWS, ROWS).transpose(2, 1, 0, 3).reshape(ROWS, N)
    )
    text_cat = every[:, :ROWS, ROWS:].transpose(1, 0, 2).reshape(ROWS, N)
    head_grads = jnp.concatenate([pose_cat, text_cat], axis=1).astype(jnp.float32)

    pose_cols = plane[:, :, ROWS:].reshape(N, ROWS)
    grad_pose = dot(pose_cols, pose_head_t, TN)
    text_cols = lax.dynamic_slice(text_rows, (0, (core * 8 + z) * ROWS), (N, ROWS))
    grad_text = dot(text_cols, text_head_t, TN)
    return (loss, grad_pose, grad_text, head_grads)


def solution(mesh):
    fine = Mesh(mesh.devices.reshape(NX, 2, NC, 2, NZ), AXES)
    placed = (P(AXES, None), P(AXES, None), P(AXES), P(), P())
    return jax.shard_map(
        local,
        mesh=fine,
        in_specs=placed,
        out_specs=(P(), P(AXES, None), P(AXES, None), P(("x", "yl", "core"), None)),
        check_vma=False,
    )
```

```python
import functools
import math

import jax
import jax.numpy as jnp
from jax import lax
from jax.experimental import pallas as pl
from jax.experimental.pallas import tpu as pltpu
from jax.sharding import Mesh
from jax.sharding import PartitionSpec as P

epsilon = 1e-06
logit_bias = -10.0
log1p_terms = (
    0.9999999403953552,
    -0.4999944567680359,
    0.3331812024116516,
    -0.2483539879322052,
    0.19076880812644958,
    -0.13602247834205627,
    0.0775160863995552,
    -0.029074065387248993,
    0.005126102361828089,
)

AXES = ("x", "yl", "core", "yh", "z")
PLANE = ("x", "yl", "yh")
LINE = ("core", "z")
NX, NY, NZ, NC = 4, 4, 8, 2
ROWS = 64
N = 1024
EXTRA = 128
TILE = 512
STEPS = N // TILE

NT = (((1,), (1,)), ((), ()))
TN = (((0,), (0,)), ((), ()))
NN = (((1,), (0,)), ((), ()))
TT = (((0,), (1,)), ((), ()))


def device_index(x, y, z, c):
    return (((x * 2 + y % 2) * 2 + c) * 2 + y // 2) * NZ + z


def pairs_of(move):
    out = []
    for x in range(NX):
        for y in range(NY):
            for z in range(NZ):
                for c in range(NC):
                    x2, y2, z2, c2 = move(x, y, z, c)
                    out.append(
                        (device_index(x, y, z, c), device_index(x2 % NX, y2 % NY, z2 % NZ, c2 % NC))
                    )
    return out


def send(value, move):
    return lax.ppermute(value, AXES, pairs_of(move))


def swap_cores(value):
    return send(value, lambda x, y, z, c: (x, y, z, 1 - c))


def plane_groups(x_core):
    groups = []
    for c in range(NC):
        for z in range(NZ):
            if c == x_core:
                groups += [[device_index(x, y, z, c) for x in range(NX)] for y in range(NY)]
            else:
                groups += [[device_index(x, y, z, c) for y in (0, 2, 1, 3)] for x in range(NX)]
    return groups


def ring_gather(shard, move, place, slot):
    rows = shard.shape[0]
    half = rows // 2
    below = send(shard, move(1))
    above = send(shard, move(-1))
    far_low = send(below[:half], move(1))
    far_high = send(above[half:], move(-1))
    out = jnp.zeros((4 * rows, shard.shape[1]), shard.dtype)
    for value, offset, start in (
        (shard, 0, 0),
        (below, 3, 0),
        (above, 1, 0),
        (far_low, 2, 0),
        (far_high, 2, half),
    ):
        at = slot((place + offset) % 4) * rows + start
        out = lax.dynamic_update_slice(out, value, (at, 0))
    return out


def along_x(by):
    return lambda x, y, z, c: (x + by, y, z, c)


def along_y(by):
    return lambda x, y, z, c: (x, y + by, z, c)


def dot(a, b, dims):
    return lax.dot_general(a, b, dims, preferred_element_type=jnp.float32)


def inverse_norm(raw):
    return lax.rsqrt(jnp.sum(raw * raw, axis=0, keepdims=True) + epsilon)


def reciprocal(value):
    guess = pltpu.reciprocal(value, approx=True)
    return guess * (2.0 - value * guess)


def back_cols(grad, unit, inverse):
    inner = jnp.sum(unit * grad, axis=0, keepdims=True)
    return ((grad - unit * inner) * inverse).astype(jnp.bfloat16)


def cols(step):
    return slice(step * TILE, (step + 1) * TILE)


def project_kernel(feats_ref, head_ref, embed_ref, unit_ref, inverse_ref):
    raw = [dot(head_ref[...], feats_ref[cols(0), :N], TT)]
    for step in range(STEPS):
        if step + 1 < STEPS:
            raw.append(dot(head_ref[...], feats_ref[cols(step + 1), :N], TT))
        inverse = inverse_norm(raw[step])
        unit = raw[step] * inverse
        unit_ref[:, cols(step)] = unit
        embed_ref[:, cols(step)] = unit.astype(jnp.bfloat16)
        inverse_ref[:, cols(step)] = jnp.broadcast_to(inverse, (8, TILE))


def pair_kernel(
    scale,
    grad_scale,
    feats_hbm,
    head_hbm,
    pose_hbm,
    pose_unit_hbm,
    pose_feats_hbm,
    pose_inverse_ref,
    target_ref,
    loss_ref,
    pose_back_hbm,
    keep_hbm,
    give_hbm,
    feats_ref,
    head_ref,
    pose_ref,
    pose_unit_ref,
    pose_feats_ref,
    text_ref,
    weights_ref,
    text_unit_ref,
    text_back_ref,
    pose_back_ref,
    pose_term_ref,
    in_sems,
    out_sems,
):
    second = lax.axis_index("core")
    out = []

    def fetch(source, target, number):
        copy = pltpu.make_async_copy(source, target, in_sems.at[number])
        copy.start()
        return copy

    def store(source, target):
        copy = pltpu.make_async_copy(source, target, out_sems.at[len(out)])
        copy.start()
        out.append(copy)

    def store_halves(source, kind, where):
        for half, target in ((second, keep_hbm), (1 - second, give_hbm)):
            store(source.at[half, :, :, where], target.at[:, kind, :, where])

    def split(value):
        return value.astype(jnp.bfloat16).reshape(2, 8, ROWS, value.shape[1])

    head_in = fetch(head_hbm, head_ref, 0)
    feats_in = [
        fetch(feats_hbm.at[cols(s), :], feats_ref.at[cols(s), :], 1 + s) for s in range(STEPS)
    ]
    pose_in = fetch(pose_hbm, pose_ref, 1 + STEPS)
    unit_in = fetch(pose_unit_hbm, pose_unit_ref, 2 + STEPS)
    pose_feats_in = fetch(pose_feats_hbm.at[:, :N], pose_feats_ref, 3 + STEPS)

    raws = []
    head_in.wait()
    for step in range(STEPS):
        feats_in[step].wait()
        raws.append(dot(head_ref[...], feats_ref[cols(step), :], TT))
    inverses = []
    for step in range(STEPS):
        inverses.append(inverse_norm(raws[step]))
        unit = raws[step] * inverses[step]
        text_unit_ref[:, cols(step)] = unit
        text_ref[:, cols(step)] = unit.astype(jnp.bfloat16)

    pose_in.wait()
    target = target_ref[0:1, :]
    inner = [dot(text_ref[:, cols(0)], pose_ref[...], TN)]
    loss_sum = None
    text_grads = []
    for step in range(STEPS):
        if step + 1 < STEPS:
            inner.append(dot(text_ref[:, cols(step + 1)], pose_ref[...], TN))
        logits = scale * inner[step] + logit_bias
        ids = lax.broadcasted_iota(jnp.int32, (TILE, 1), 0) + step * TILE
        paired = ids == target
        arg = jnp.where(paired, -logits, logits)
        small = jnp.exp(-jnp.abs(arg))
        sig = jnp.where(arg >= 0.0, 1.0, small) * reciprocal(1.0 + small)
        weights_ref[cols(step), :] = (jnp.where(paired, -grad_scale, grad_scale) * sig).astype(
            jnp.bfloat16
        )
        poly = jnp.full_like(small, log1p_terms[-1])
        for term in log1p_terms[-2::-1]:
            poly = poly * small + term
        loss = jnp.maximum(arg, 0.0) + small * poly
        part = jnp.sum(loss.reshape(TILE // 8, 8, N), axis=0)
        loss_sum = part if loss_sum is None else loss_sum + part
        text_grads.append(dot(pose_ref[...], weights_ref[cols(step), :], NT))
    loss_ref[...] = loss_sum

    unit_in.wait()
    pose_grads = [dot(text_ref[...], weights_ref[:, cols(0)], NN)]
    for step in range(STEPS):
        if step + 1 < STEPS:
            pose_grads.append(dot(text_ref[...], weights_ref[:, cols(step + 1)], NN))
        text_back_ref[:, :, :, cols(step)] = split(
            back_cols(text_grads[step], text_unit_ref[:, cols(step)], inverses[step])
        )
        store_halves(text_back_ref, 0, cols(step))
    for step in range(STEPS):
        pose_back_ref[:, cols(step)] = back_cols(
            pose_grads[step], pose_unit_ref[:, cols(step)], pose_inverse_ref[0:1, cols(step)]
        )
        for block in range(16):
            to = block + second * (block % 4 * 4 + block // 4 - block)
            store(
                pose_back_ref.at[block * ROWS : (block + 1) * ROWS, cols(step)],
                pose_back_hbm.at[pl.ds(pl.multiple_of(to * ROWS, ROWS), ROWS), cols(step)],
            )
    pose_feats_in.wait()
    for step in range(STEPS):
        pose_term_ref[:, :, :, cols(step)] = split(
            dot(pose_back_ref[...], pose_feats_ref[:, cols(step)], NN)
        )
        store_halves(pose_term_ref, 1, cols(step))
    for copy in out:
        copy.wait()


VMEM = pl.BlockSpec(memory_space=pltpu.VMEM)
ANY = pl.BlockSpec(memory_space=pl.ANY)
LIMIT = pltpu.CompilerParams(vmem_limit_bytes=48 * 1024 * 1024)


def shape(rows, dtype):
    return jax.ShapeDtypeStruct((rows, N), dtype)


def project(feats, head_t):
    return pl.pallas_call(
        project_kernel,
        out_shape=(shape(N, jnp.bfloat16), shape(N, jnp.float32), shape(8, jnp.float32)),
        in_specs=[VMEM] * 2,
        out_specs=(VMEM,) * 3,
        compiler_params=LIMIT,
        cost_estimate=pl.CostEstimate(flops=2 * N**3, bytes_accessed=12 * N * N, transcendentals=0),
    )(feats, head_t)


def score(scale, grad_scale, feats, head, pose, pose_unit, pose_feats, pose_inverse, target):
    half = pltpu.VMEM((N, N), jnp.bfloat16)
    full = pltpu.VMEM((N, N), jnp.float32)
    blocks = pltpu.VMEM((2, 8, ROWS, N), jnp.bfloat16)
    return pl.pallas_call(
        functools.partial(pair_kernel, scale, grad_scale),
        out_shape=(
            shape(8, jnp.float32),
            shape(N, jnp.bfloat16),
            jax.ShapeDtypeStruct((8, 2, ROWS, N), jnp.bfloat16),
            jax.ShapeDtypeStruct((8, 2, ROWS, N), jnp.bfloat16),
        ),
        in_specs=[ANY] * 5 + [VMEM] * 2,
        out_specs=(VMEM, ANY, ANY, ANY),
        scratch_shapes=[
            half,
            half,
            half,
            full,
            half,
            half,
            half,
            full,
            blocks,
            half,
            blocks,
            pltpu.SemaphoreType.DMA((4 + STEPS,)),
            pltpu.SemaphoreType.DMA((20 * STEPS,)),
        ],
        compiler_params=LIMIT,
        cost_estimate=pl.CostEstimate(
            flops=10 * N**3, bytes_accessed=20 * N * N, transcendentals=2 * N * N
        ),
    )(feats, head, pose, pose_unit, pose_feats, pose_inverse, target)


def loss_block(value):
    high = lax.reduce_precision(value, 8, 7)
    middle = lax.reduce_precision(value - high, 8, 7)
    low = value - high - middle
    rows = lax.broadcasted_iota(jnp.int32, (16, 2 * ROWS), 0)
    block = jnp.where(rows == 0, high, jnp.where(rows == 1, middle, jnp.where(rows == 2, low, 0.0)))
    return jnp.broadcast_to(block.astype(jnp.bfloat16)[None], (16, 16, 2 * ROWS))


def sum_loss(blocks):
    return jnp.sum(blocks[:, -16:-13, 0].astype(jnp.float32))


def fold(blocks):
    return jnp.concatenate([blocks[:, : ROWS // 2], blocks[:, ROWS // 2 :]], axis=2)


def unfold(blocks):
    return jnp.concatenate([blocks[:, :, :ROWS], blocks[:, :, ROWS:]], axis=1)


def local(pose_feats, text_feats, match, pose_head, text_head):
    batch_size = ROWS * 256
    logit_scale = 2.0 * math.sqrt(N)
    grad_scale = logit_scale / math.sqrt(batch_size)
    x = lax.axis_index("x")
    yl = lax.axis_index("yl")
    yh = lax.axis_index("yh")

    text_group = lax.all_gather(text_feats, LINE, axis=0, tiled=True)
    ids = jnp.stack([match // 128, match % 128], axis=1).astype(jnp.bfloat16)
    shard = jnp.concatenate([pose_feats, jnp.pad(ids, ((0, 0), (0, EXTRA - 2)))], axis=1)
    pose_group = ring_gather(shard, along_y, yh * 2 + yl, lambda y: y % 2 * 2 + y // 2)
    pose_group = ring_gather(pose_group, along_x, x, lambda x: x)
    pose, pose_unit, pose_inverse = project(pose_group, pose_head)
    lanes = lax.broadcasted_iota(jnp.int32, (8, EXTRA), 1)
    pick = jnp.where(lanes == 0, 128.0, jnp.where(lanes == 1, 1.0, 0.0)).astype(jnp.bfloat16)
    group_ids = dot(pick, pose_group[:, N:], NT).astype(jnp.int32)
    offset = group_ids - ((x * 2 + yl) * 2048 + yh * 512)
    inside = (offset >= 0) & (offset < 2048) & (offset % 1024 < 512)
    target = jnp.where(inside, offset // 1024 * 512 + offset % 1024, -1)

    loss_part, pose_part, keep, give = score(
        logit_scale,
        grad_scale,
        text_group,
        text_head,
        pose,
        pose_unit,
        pose_group,
        pose_inverse,
        target,
    )
    got = swap_cores(give)
    both = (keep.astype(jnp.float32) + got.astype(jnp.float32)).astype(jnp.bfloat16)
    both, pose_part = lax.optimization_barrier((both, pose_part))
    both = lax.psum_scatter(both, "z", scatter_dimension=0, tiled=True)
    text_back, pose_term = both[0, 0], both[0, 1]

    parts = lax.all_to_all(
        pose_part.reshape(4, 4 * ROWS, N), AXES, 0, 0, axis_index_groups=plane_groups(0)
    )
    pose_sum = jnp.sum(parts.astype(jnp.float32), axis=0).astype(jnp.bfloat16)
    parts = lax.all_to_all(
        pose_sum.reshape(4, ROWS, N), AXES, 0, 0, axis_index_groups=plane_groups(1)
    )
    pose_back = jnp.sum(parts.astype(jnp.float32), axis=0).astype(jnp.bfloat16)
    pose_rows = fold(pose_back.reshape(ROWS, 16, ROWS).transpose(1, 0, 2))

    text_term = jnp.dot(text_back, text_group, preferred_element_type=jnp.float32)
    terms = jnp.stack([pose_term, text_term.astype(jnp.bfloat16)])
    terms = terms.reshape(2 * ROWS, 8, 2 * ROWS).transpose(1, 0, 2)
    terms = jnp.broadcast_to(terms[:, None], (8, 2, 2 * ROWS, 2 * ROWS))
    terms = terms.reshape(16, 2 * ROWS, 2 * ROWS)
    plane = lax.all_to_all(
        jnp.concatenate([terms, pose_rows, loss_block(jnp.sum(loss_part))], axis=1), PLANE, 0, 0
    )
    sums = jnp.sum(plane[:, : 2 * ROWS].astype(jnp.float32), axis=0).astype(jnp.bfloat16)
    pose_cols = unfold(plane[:, 2 * ROWS : 2 * ROWS + ROWS // 2]).reshape(N, ROWS)

    turned = sums.reshape(2, ROWS, 2, ROWS).transpose(2, 3, 0, 1).reshape(2, ROWS, 2 * ROWS)
    turned = jnp.broadcast_to(turned[:, None], (2, 8, ROWS, 2 * ROWS)).reshape(16, ROWS, 2 * ROWS)
    text_rows = fold(text_back.reshape(ROWS, 16, ROWS).transpose(1, 0, 2))
    line = lax.all_to_all(
        jnp.concatenate([turned, text_rows, loss_block(sum_loss(plane))], axis=1), LINE, 0, 0
    )
    loss = sum_loss(line) / (batch_size * batch_size)
    heads = line[:, :ROWS].reshape(16, ROWS, 2, ROWS).transpose(1, 2, 0, 3)
    head_grads = heads.reshape(ROWS, 2 * N).astype(jnp.float32)
    text_cols = unfold(line[:, ROWS : ROWS + ROWS // 2]).reshape(N, ROWS)

    grad_pose = dot(pose_cols.T, pose_head, NT)
    grad_text = dot(text_cols.T, text_head, NT)
    return (loss, grad_pose, grad_text, head_grads)


def solution(mesh):
    fine = Mesh(mesh.devices.reshape(NX, 2, NC, 2, NZ), AXES)
    placed = (P(AXES, None), P(AXES, None), P(AXES), P(), P())
    return jax.shard_map(
        local,
        mesh=fine,
        in_specs=placed,
        out_specs=(P(), P(AXES, None), P(AXES, None), P(("x", "yl", "core"), None)),
        check_vma=False,
    )
```

```python
import functools
import math

import jax
import jax.numpy as jnp
from jax import lax
from jax.experimental import pallas as pl
from jax.experimental.pallas import tpu as pltpu
from jax.sharding import Mesh
from jax.sharding import PartitionSpec as P

epsilon = 1e-06
logit_bias = -10.0
log1p_terms = (
    0.9999999403953552,
    -0.4999944567680359,
    0.3331812024116516,
    -0.2483539879322052,
    0.19076880812644958,
    -0.13602247834205627,
    0.0775160863995552,
    -0.029074065387248993,
    0.005126102361828089,
)

AXES = ("x", "yl", "core", "yh", "z")
PLANE = ("x", "yl", "yh")
LINE = ("core", "z")
NX, NY, NZ, NC = 4, 4, 8, 2
ROWS = 64
N = 1024
EXTRA = 128
TILE = 512
STEPS = N // TILE

NT = (((1,), (1,)), ((), ()))
TN = (((0,), (0,)), ((), ()))
NN = (((1,), (0,)), ((), ()))
TT = (((0,), (1,)), ((), ()))


def device_index(x, y, z, c):
    return (((x * 2 + y % 2) * 2 + c) * 2 + y // 2) * NZ + z


def pairs_of(move):
    out = []
    for x in range(NX):
        for y in range(NY):
            for z in range(NZ):
                for c in range(NC):
                    x2, y2, z2, c2 = move(x, y, z, c)
                    out.append(
                        (device_index(x, y, z, c), device_index(x2 % NX, y2 % NY, z2 % NZ, c2 % NC))
                    )
    return out


def send(value, move):
    return lax.ppermute(value, AXES, pairs_of(move))


def swap_cores(value):
    return send(value, lambda x, y, z, c: (x, y, z, 1 - c))


def ring_pieces(shard, move):
    half = shard.shape[0] // 2
    below = send(shard, move(1))
    above = send(shard, move(-1))
    far_low = send(below[:half], move(1))
    far_high = send(above[half:], move(-1))
    return ((shard, 0, 0), (below, 3, 0), (above, 1, 0), (far_low, 2, 0), (far_high, 2, half))


def place_pieces(pieces, place, slot):
    rows = pieces[0][0].shape[0]
    out = jnp.zeros((4 * rows, pieces[0][0].shape[1]), pieces[0][0].dtype)
    for value, offset, start in pieces:
        at = slot((place + offset) % 4) * rows + start
        out = lax.dynamic_update_slice(out, value, (at, 0))
    return out


def along_x(by):
    return lambda x, y, z, c: (x + by, y, z, c)


def along_y(by):
    return lambda x, y, z, c: (x, y + by, z, c)


def dot(a, b, dims):
    return lax.dot_general(a, b, dims, preferred_element_type=jnp.float32)


def inverse_norm(raw):
    return lax.rsqrt(jnp.sum(raw * raw, axis=0, keepdims=True) + epsilon)


def reciprocal(value):
    guess = pltpu.reciprocal(value, approx=True)
    return guess * (2.0 - value * guess)


def back_cols(grad, unit, inverse):
    inner = jnp.sum(unit * grad, axis=0, keepdims=True)
    return ((grad - unit * inner) * inverse).astype(jnp.bfloat16)


def cols(step):
    return slice(step * TILE, (step + 1) * TILE)


def pair_kernel(
    scale,
    grad_scale,
    near_hbm,
    below_hbm,
    above_hbm,
    far_low_hbm,
    far_high_hbm,
    pose_head_hbm,
    text_own_hbm,
    text_other_hbm,
    text_head_hbm,
    loss_ref,
    pose_rows_hbm,
    keep_hbm,
    give_hbm,
    pose_feats_ref,
    pose_head_ref,
    text_feats_ref,
    text_head_ref,
    pose_ref,
    pose_unit_ref,
    text_ref,
    text_unit_ref,
    weights_ref,
    text_back_ref,
    pose_back_ref,
    pose_rows_ref,
    pose_term_ref,
    in_sems,
    out_sems,
):
    second = lax.axis_index("core")
    out = []

    def fetch(source, target, number):
        copy = pltpu.make_async_copy(source, target, in_sems.at[number])
        copy.start()
        return copy

    def store(source, target):
        copy = pltpu.make_async_copy(source, target, out_sems.at[len(out)])
        copy.start()
        out.append(copy)

    def store_halves(source, kind, where):
        for half, target in ((second, keep_hbm), (1 - second, give_hbm)):
            for block in range(NZ):
                to = lax.rem(block + NZ - lax.axis_index("z"), NZ)
                store(source.at[half, block, :, where], target.at[to, kind, :, where])

    def split(value):
        return value.astype(jnp.bfloat16).reshape(2, 8, ROWS, value.shape[1])

    def half_rows(half):
        return pl.ds(pl.multiple_of(half * (N // 2), N // 2), N // 2)

    pose_head_in = fetch(pose_head_hbm, pose_head_ref, 0)
    pose_in = []
    for source, offset, start in (
        (near_hbm, 0, 0),
        (below_hbm, 3, 0),
        (above_hbm, 1, 0),
        (far_low_hbm, 2, 0),
        (far_high_hbm, 2, N // 8),
    ):
        at = lax.rem(lax.axis_index("x") + offset, 4) * (N // 4) + start
        at = pl.multiple_of(at, N // 8)
        target = pose_feats_ref.at[pl.ds(at, source.shape[0]), :]
        pose_in.append(fetch(source, target, 1 + len(pose_in)))
    text_head_in = fetch(text_head_hbm, text_head_ref, 6)
    own_in = fetch(text_own_hbm, text_feats_ref.at[half_rows(second), :], 7)
    other_in = fetch(text_other_hbm, text_feats_ref.at[half_rows(1 - second), :], 8)

    pose_raws, text_raws = [], []
    pose_head_in.wait()
    for copy in pose_in:
        copy.wait()
    for step in range(STEPS):
        pose_raws.append(dot(pose_head_ref[...], pose_feats_ref[cols(step), :N], TT))
    text_head_in.wait()
    own_in.wait()
    other_in.wait()
    pose_inverses, text_inverses = [], []
    for step in range(STEPS):
        text_raws.append(dot(text_head_ref[...], text_feats_ref[cols(step), :], TT))
        pose_inverses.append(inverse_norm(pose_raws[step]))
        unit = pose_raws[step] * pose_inverses[step]
        pose_unit_ref[:, cols(step)] = unit
        pose_ref[:, cols(step)] = unit.astype(jnp.bfloat16)
    for step in range(STEPS):
        text_inverses.append(inverse_norm(text_raws[step]))
        unit = text_raws[step] * text_inverses[step]
        text_unit_ref[:, cols(step)] = unit
        text_ref[:, cols(step)] = unit.astype(jnp.bfloat16)

    lanes = lax.broadcasted_iota(jnp.int32, (8, EXTRA), 1)
    pick = jnp.where(lanes == 0, 128.0, jnp.where(lanes == 1, 1.0, 0.0)).astype(jnp.bfloat16)
    match = dot(pick, pose_feats_ref[:, N:], NT).astype(jnp.int32)[0:1, :]
    place = lax.axis_index("x") * 2 + lax.axis_index("yl")
    offset = match - (place * 2048 + lax.axis_index("yh") * 512)
    late = offset >= 1024
    within = jnp.where(late, offset - 1024, offset)
    inside = (within >= 0) & (within < 512)
    target = jnp.where(inside, within + jnp.where(late, 512, 0), -1)

    inner = [dot(text_ref[:, cols(0)], pose_ref[...], TN)]
    loss_sum = None
    text_grads = []
    for step in range(STEPS):
        if step + 1 < STEPS:
            inner.append(dot(text_ref[:, cols(step + 1)], pose_ref[...], TN))
        logits = scale * inner[step] + logit_bias
        ids = lax.broadcasted_iota(jnp.int32, (TILE, 1), 0) + step * TILE
        paired = ids == target
        arg = jnp.where(paired, -logits, logits)
        small = jnp.exp(-jnp.abs(arg))
        sig = jnp.where(arg >= 0.0, 1.0, small) * reciprocal(1.0 + small)
        weights_ref[cols(step), :] = (jnp.where(paired, -grad_scale, grad_scale) * sig).astype(
            jnp.bfloat16
        )
        poly = jnp.full_like(small, log1p_terms[-1])
        for term in log1p_terms[-2::-1]:
            poly = poly * small + term
        loss = jnp.maximum(arg, 0.0) + small * poly
        part = jnp.sum(loss.reshape(TILE // 8, 8, N), axis=0)
        loss_sum = part if loss_sum is None else loss_sum + part
        text_grads.append(dot(pose_ref[...], weights_ref[cols(step), :], NT))
    loss_ref[...] = loss_sum

    pose_grads = [dot(text_ref[...], weights_ref[:, cols(0)], NN)]
    for step in range(STEPS):
        if step + 1 < STEPS:
            pose_grads.append(dot(text_ref[...], weights_ref[:, cols(step + 1)], NN))
        text_back_ref[:, :, :, cols(step)] = split(
            back_cols(text_grads[step], text_unit_ref[:, cols(step)], text_inverses[step])
        )
        store_halves(text_back_ref, 0, cols(step))
    for step in range(STEPS):
        back = back_cols(pose_grads[step], pose_unit_ref[:, cols(step)], pose_inverses[step])
        pose_back_ref[:, cols(step)] = back
    for step in range(STEPS):
        pose_term_ref[:, :, :, cols(step)] = split(
            dot(pose_back_ref[...], pose_feats_ref[:, cols(step)], NN)
        )
        store_halves(pose_term_ref, 1, cols(step))
        pose_rows_ref[cols(step), :] = pose_back_ref[:, cols(step)].T
        store(pose_rows_ref.at[cols(step), :], pose_rows_hbm.at[cols(step), :])
    for copy in out:
        copy.wait()


def loss_block(value):
    high = value.astype(jnp.bfloat16)
    rest = value - high.astype(jnp.float32)
    middle = rest.astype(jnp.bfloat16)
    low = (rest - middle.astype(jnp.float32)).astype(jnp.bfloat16)
    rows = lax.broadcasted_iota(jnp.int32, (16, 2 * ROWS), 0)
    block = jnp.where(
        rows == 0,
        high.astype(jnp.float32),
        jnp.where(
            rows == 1,
            middle.astype(jnp.float32),
            jnp.where(rows == 2, low.astype(jnp.float32), 0.0),
        ),
    )
    return block.astype(jnp.bfloat16)


def sum_loss(blocks):
    sums = jnp.sum(blocks.astype(jnp.float32), axis=0)
    return jnp.sum(sums[:3], axis=0, keepdims=True)


def terms_kernel(both_ref, own_ref, other_ref, loss_ref, out_ref):
    second = lax.axis_index("core")

    def text_cols(half):
        return both_ref[:ROWS, pl.ds(pl.multiple_of(half * (N // 2), N // 2), N // 2)]

    text_term = dot(text_cols(second), own_ref[...], NN)
    text_term += dot(text_cols(1 - second), other_ref[...], NN)
    text_term = text_term.astype(jnp.bfloat16)
    block = loss_block(jnp.full((16, 2 * ROWS), jnp.sum(loss_ref[...]), jnp.float32))
    for place in range(8):
        where = slice(place * 2 * ROWS, (place + 1) * 2 * ROWS)
        for high in range(2):
            out_ref[place * 2 + high, :ROWS, :] = both_ref[ROWS:, where]
            out_ref[place * 2 + high, ROWS : 2 * ROWS, :] = text_term[:, where]
            out_ref[place * 2 + high, 2 * ROWS :, :] = block


def turn_kernel(plane_ref, rows_ref, out_ref):
    sums = jnp.sum(plane_ref[:, : 2 * ROWS, :].astype(jnp.float32), axis=0).T.astype(jnp.bfloat16)
    total = sum_loss(plane_ref[:, 2 * ROWS :, :])
    block = loss_block(jnp.broadcast_to(total, (16, 2 * ROWS)))
    for core in range(NC):
        for z in range(NZ):
            out_ref[core * NZ + z, :ROWS, :] = sums[core * ROWS : (core + 1) * ROWS]
            out_ref[core * NZ + z, ROWS : ROWS + 32, :] = rows_ref[core * NZ + z]
            out_ref[core * NZ + z, ROWS + 32 :, :] = block


def last_kernel(line_ref, head_ref, grad_ref, heads_ref, loss_ref, text_ref):
    for m in range(16):
        text_ref[m * ROWS : m * ROWS + 32, :] = line_ref[m, ROWS : ROWS + 32, :ROWS]
        text_ref[m * ROWS + 32 : (m + 1) * ROWS, :] = line_ref[m, ROWS : ROWS + 32, ROWS:]
    grad_ref[...] = dot(text_ref[...], head_ref[...], TT)
    for m in range(0, 16, 2):
        for kind in range(2):
            lanes = slice(kind * ROWS, (kind + 1) * ROWS)
            pair = [line_ref[m + i, :ROWS, lanes].astype(jnp.float32) for i in range(2)]
            heads_ref[:, kind * N + m * ROWS : kind * N + (m + 2) * ROWS] = jnp.concatenate(
                pair, axis=1
            )
    total = sum_loss(line_ref[:, ROWS + 32 :, :]) / float(N * 16) ** 2
    loss_ref[...] = jnp.broadcast_to(total, (8, 2 * ROWS))


VMEM = pl.BlockSpec(memory_space=pltpu.VMEM)
ANY = pl.BlockSpec(memory_space=pl.ANY)


def shape(rows, dtype):
    return jax.ShapeDtypeStruct((rows, N), dtype)


def score(scale, grad_scale, pose_pieces, pose_head, text_own, text_other, text_head):
    half = pltpu.VMEM((N, N), jnp.bfloat16)
    full = pltpu.VMEM((N, N), jnp.float32)
    blocks = pltpu.VMEM((2, 8, ROWS, N), jnp.bfloat16)
    return pl.pallas_call(
        functools.partial(pair_kernel, scale, grad_scale),
        out_shape=(
            shape(8, jnp.float32),
            shape(N, jnp.bfloat16),
            jax.ShapeDtypeStruct((8, 2, ROWS, N), jnp.bfloat16),
            jax.ShapeDtypeStruct((8, 2, ROWS, N), jnp.bfloat16),
        ),
        in_specs=[ANY] * 9,
        out_specs=(VMEM, ANY, ANY, ANY),
        scratch_shapes=[
            pltpu.VMEM((N, N + EXTRA), jnp.bfloat16),
            half,
            half,
            half,
            half,
            full,
            half,
            full,
            half,
            blocks,
            half,
            half,
            blocks,
            pltpu.SemaphoreType.DMA((9,)),
            pltpu.SemaphoreType.DMA(((4 * NZ + 1) * STEPS,)),
        ],
        compiler_params=pltpu.CompilerParams(vmem_limit_bytes=44 * 1024 * 1024),
        cost_estimate=pl.CostEstimate(
            flops=12 * N**3, bytes_accessed=20 * N * N, transcendentals=2 * N * N
        ),
    )(*pose_pieces, pose_head, text_own, text_other, text_head)


def small_call(kernel, out_shape, scratch, *args):
    return pl.pallas_call(
        kernel,
        out_shape=out_shape,
        in_specs=[VMEM] * len(args),
        out_specs=jax.tree.map(lambda _: VMEM, out_shape),
        scratch_shapes=scratch,
        compiler_params=pltpu.CompilerParams(vmem_limit_bytes=16 * 1024 * 1024),
        cost_estimate=pl.CostEstimate(
            flops=2 * ROWS * N * N, bytes_accessed=4 * N * N, transcendentals=0
        ),
    )(*args)


def fold(blocks):
    return jnp.concatenate([blocks[:, : ROWS // 2], blocks[:, ROWS // 2 :]], axis=2)


def along_z(by):
    return lambda x, y, z, c: (x, y, z + by, c)


def ring_sum(keep, got):
    half = keep.shape[1] // 2

    def own(by):
        return keep[by % NZ].astype(jnp.float32) + got[by % NZ].astype(jnp.float32)

    def bf(value):
        return value.astype(jnp.bfloat16)

    up = send(bf(own(4)[:half]), along_z(1))
    down = send(bf(own(4)[half:]), along_z(-1))
    for by in (3, 2, 1):
        upper, lower = own(by), own(-by)
        if by == 3:
            up = jnp.concatenate([upper[:half] + up.astype(jnp.float32), upper[half:]])
            down = jnp.concatenate([lower[:half], lower[half:] + down.astype(jnp.float32)])
        else:
            up = upper + up.astype(jnp.float32)
            down = lower + down.astype(jnp.float32)
        up = send(bf(up), along_z(1))
        down = send(bf(down), along_z(-1))
    return bf(own(0) + up.astype(jnp.float32) + down.astype(jnp.float32))


def repeat_kernel(rows_ref, out_ref):
    for block in range(NZ):
        out_ref[block] = rows_ref[...]


def local(pose_feats, text_feats, match, pose_head, text_head):
    batch_size = ROWS * 256
    logit_scale = 2.0 * math.sqrt(N)
    grad_scale = logit_scale / math.sqrt(batch_size)
    yl = lax.axis_index("yl")
    yh = lax.axis_index("yh")

    text_own = lax.all_to_all(
        small_call(repeat_kernel, jax.ShapeDtypeStruct((NZ, ROWS, N), jnp.bfloat16), [], text_feats),
        "z",
        0,
        0,
    )
    text_own = text_own.reshape(NZ * ROWS, N)
    ids = jnp.stack([match // 128, match % 128], axis=1).astype(jnp.bfloat16)
    shard = jnp.concatenate([pose_feats, jnp.pad(ids, ((0, 0), (0, EXTRA - 2)))], axis=1)
    column = place_pieces(
        ring_pieces(shard, along_y), yh * 2 + yl, lambda y: y % 2 * 2 + y // 2
    )
    pieces = [piece for piece, _, _ in ring_pieces(column, along_x)]
    text_own, pieces[1], pieces[2] = lax.optimization_barrier((text_own, pieces[1], pieces[2]))
    text_other = swap_cores(text_own)

    loss_part, pose_part, keep, give = score(
        logit_scale, grad_scale, pieces, pose_head, text_own, text_other, text_head
    )
    got = swap_cores(give)
    got, pose_part = lax.optimization_barrier((got, pose_part))
    pose_parts = lax.all_to_all(pose_part.reshape(16, ROWS, N), PLANE, 0, 0)
    both = ring_sum(keep.reshape(NZ, 2 * ROWS, N), got.reshape(NZ, 2 * ROWS, N))

    both, pose_parts = lax.optimization_barrier((both, pose_parts))
    pose_back = jnp.sum(pose_parts.astype(jnp.float32), axis=0).astype(jnp.bfloat16)
    grad_pose = dot(pose_back, pose_head, NT)

    bf16 = jnp.bfloat16
    terms = small_call(
        terms_kernel,
        jax.ShapeDtypeStruct((16, 2 * ROWS + 16, 2 * ROWS), bf16),
        [],
        both,
        text_own,
        text_other,
        loss_part,
    )
    plane = lax.all_to_all(terms, PLANE, 0, 0)
    text_rows = fold(both[:ROWS].reshape(ROWS, 16, ROWS).transpose(1, 0, 2))
    turned = small_call(
        turn_kernel,
        jax.ShapeDtypeStruct((16, ROWS + 48, 2 * ROWS), bf16),
        [],
        plane,
        text_rows,
    )
    line = lax.all_to_all(turned, LINE, 0, 0)
    grad_text, head_grads, loss = small_call(
        last_kernel,
        (
            shape(ROWS, jnp.float32),
            jax.ShapeDtypeStruct((ROWS, 2 * N), jnp.float32),
            jax.ShapeDtypeStruct((8, 2 * ROWS), jnp.float32),
        ),
        [pltpu.VMEM((N, ROWS), bf16)],
        line,
        text_head,
    )
    return (loss[0, 0], grad_pose, grad_text, head_grads)


def solution(mesh):
    fine = Mesh(mesh.devices.reshape(NX, 2, NC, 2, NZ), AXES)
    placed = (P(AXES, None), P(AXES, None), P(AXES), P(), P())
    return jax.shard_map(
        local,
        mesh=fine,
        in_specs=placed,
        out_specs=(P(), P(AXES, None), P(AXES, None), P(("x", "yl", "core"), None)),
        check_vma=False,
    )
```

```python
import functools
import math

import jax
import jax.numpy as jnp
from jax import lax
from jax.experimental import pallas as pl
from jax.experimental.pallas import tpu as pltpu
from jax.sharding import Mesh
from jax.sharding import PartitionSpec as P

epsilon = 1e-06
logit_bias = -10.0
log1p_terms = (
    0.9999997615814209,
    -0.49997174739837646,
    0.3327192962169647,
    -0.24474774301052094,
    0.1768747717142105,
    -0.1068500280380249,
    0.04349390044808388,
    -0.00837115291506052,
)

AXES = ("x", "yl", "core", "yh", "z")
PLANE = ("x", "yl", "yh")
LINE = ("core", "z")
NX, NY, NZ, NC = 4, 4, 8, 2
ROWS = 64
N = 1024
EXTRA = 128
TILE = 512
STEPS = N // TILE

NT = (((1,), (1,)), ((), ()))
TN = (((0,), (0,)), ((), ()))
NN = (((1,), (0,)), ((), ()))
TT = (((0,), (1,)), ((), ()))


def device_index(x, y, z, c):
    return (((x * 2 + y % 2) * 2 + c) * 2 + y // 2) * NZ + z


def pairs_of(move):
    out = []
    for x in range(NX):
        for y in range(NY):
            for z in range(NZ):
                for c in range(NC):
                    x2, y2, z2, c2 = move(x, y, z, c)
                    out.append(
                        (device_index(x, y, z, c), device_index(x2 % NX, y2 % NY, z2 % NZ, c2 % NC))
                    )
    return out


def send(value, move):
    return lax.ppermute(value, AXES, pairs_of(move))


def swap_cores(value):
    return send(value, lambda x, y, z, c: (x, y, z, 1 - c))


def ring_pieces(shard, move):
    half = shard.shape[0] // 2
    below = send(shard, move(1))
    above = send(shard, move(-1))
    far_low = send(below[:half], move(1))
    far_high = send(above[half:], move(-1))
    return ((shard, 0, 0), (below, 3, 0), (above, 1, 0), (far_low, 2, 0), (far_high, 2, half))


def plane_move(x_core):
    def move_by(by):
        def move(x, y, z, c):
            return (x + by, y, z, c) if c == x_core else (x, y + by, z, c)

        return move

    return move_by


def y_slot(y):
    return y % 2 * 2 + y // 2


def dot(a, b, dims):
    return lax.dot_general(a, b, dims, preferred_element_type=jnp.float32)


def inverse_norm(raw):
    return lax.rsqrt(jnp.sum(raw * raw, axis=0, keepdims=True) + epsilon)


def reciprocal(value):
    guess = pltpu.reciprocal(value, approx=True)
    return guess * (2.0 - value * guess)


def back_cols(grad, unit, inverse):
    inner = jnp.sum(unit * grad, axis=0, keepdims=True)
    return ((grad - unit * inner) * inverse).astype(jnp.bfloat16)


def cols(step):
    return slice(step * TILE, (step + 1) * TILE)


def pair_kernel(
    scale,
    grad_scale,
    near_hbm,
    below_hbm,
    above_hbm,
    far_low_hbm,
    far_high_hbm,
    pose_head_hbm,
    text_own_hbm,
    text_other_hbm,
    text_head_hbm,
    loss_ref,
    pose_rows_hbm,
    keep_hbm,
    give_hbm,
    pose_feats_ref,
    pose_head_ref,
    text_feats_ref,
    text_head_ref,
    pose_ref,
    pose_unit_ref,
    text_ref,
    text_unit_ref,
    weights_ref,
    text_back_ref,
    pose_back_ref,
    pose_rows_ref,
    pose_term_ref,
    in_sems,
    out_sems,
):
    second = lax.axis_index("core")
    out = []

    def fetch(source, target, number):
        copy = pltpu.make_async_copy(source, target, in_sems.at[number])
        copy.start()
        return copy

    def store(source, target):
        copy = pltpu.make_async_copy(source, target, out_sems.at[len(out)])
        copy.start()
        out.append(copy)

    def store_halves(source, kind, where):
        for half, target in ((second, keep_hbm), (1 - second, give_hbm)):
            for block in range(NZ):
                to = lax.rem(block + NZ - lax.axis_index("z"), NZ)
                store(source.at[half, block, :, where], target.at[to, kind, :, where])

    def split(value):
        return value.astype(jnp.bfloat16).reshape(2, 8, ROWS, value.shape[1])

    def half_rows(half):
        return pl.ds(pl.multiple_of(half * (N // 2), N // 2), N // 2)

    pose_head_in = fetch(pose_head_hbm, pose_head_ref, 0)
    pose_in = []
    x, y = lax.axis_index("x"), lax.axis_index("yh") * 2 + lax.axis_index("yl")
    for source, offset, first in (
        (near_hbm, 0, 0),
        (below_hbm, 3, 0),
        (above_hbm, 1, 0),
        (far_low_hbm, 2, 0),
        (far_high_hbm, 2, 2),
    ):
        x_at = lax.rem(x + offset, 4)
        y_at = lax.rem(y + offset, 4)
        y_at = lax.rem(y_at, 2) * 2 + y_at // 2
        for block in range(source.shape[0] // ROWS):
            place = jnp.where(second == 0, x_at * 4 + first + block, (first + block) * 4 + y_at)
            at = pl.multiple_of(place * ROWS, ROWS)
            pose_in.append(
                fetch(
                    source.at[block * ROWS : (block + 1) * ROWS, :],
                    pose_feats_ref.at[pl.ds(at, ROWS), :],
                    1 + len(pose_in),
                )
            )
    text_head_in = fetch(text_head_hbm, text_head_ref, 17)
    own_in = fetch(text_own_hbm, text_feats_ref.at[half_rows(second), :], 18)
    other_in = fetch(text_other_hbm, text_feats_ref.at[half_rows(1 - second), :], 19)

    pose_raws, text_raws = [], []
    pose_head_in.wait()
    for copy in pose_in:
        copy.wait()
    for step in range(STEPS):
        pose_raws.append(dot(pose_head_ref[...], pose_feats_ref[cols(step), :N], TT))
    text_head_in.wait()
    own_in.wait()
    other_in.wait()
    pose_inverses, text_inverses = [], []
    for step in range(STEPS):
        text_raws.append(dot(text_head_ref[...], text_feats_ref[cols(step), :], TT))
        pose_inverses.append(inverse_norm(pose_raws[step]))
        unit = pose_raws[step] * pose_inverses[step]
        pose_unit_ref[:, cols(step)] = unit
        pose_ref[:, cols(step)] = unit.astype(jnp.bfloat16)
    for step in range(STEPS):
        text_inverses.append(inverse_norm(text_raws[step]))
        unit = text_raws[step] * text_inverses[step]
        text_unit_ref[:, cols(step)] = unit
        text_ref[:, cols(step)] = unit.astype(jnp.bfloat16)

    lanes = lax.broadcasted_iota(jnp.int32, (8, EXTRA), 1)
    pick = jnp.where(lanes == 0, 128.0, jnp.where(lanes == 1, 1.0, 0.0)).astype(jnp.bfloat16)
    match = dot(pick, pose_feats_ref[:, N:], NT).astype(jnp.int32)[0:1, :]
    place = lax.axis_index("x") * 2 + lax.axis_index("yl")
    offset = match - (place * 2048 + lax.axis_index("yh") * 512)
    late = offset >= 1024
    within = jnp.where(late, offset - 1024, offset)
    inside = (within >= 0) & (within < 512)
    target = jnp.where(inside, within + jnp.where(late, 512, 0), -1)

    inner = [dot(text_ref[:, cols(0)], pose_ref[...], TN)]
    loss_sum = None
    text_grads = []
    for step in range(STEPS):
        if step + 1 < STEPS:
            inner.append(dot(text_ref[:, cols(step + 1)], pose_ref[...], TN))
        logits = scale * inner[step] + logit_bias
        ids = lax.broadcasted_iota(jnp.int32, (TILE, 1), 0) + step * TILE
        paired = ids == target
        positive = paired != (logits >= 0.0)
        size = jnp.abs(logits)
        small = jnp.exp(-size)
        sig = jnp.where(positive, 1.0, small) * reciprocal(1.0 + small)
        weights_ref[cols(step), :] = (jnp.where(paired, -grad_scale, grad_scale) * sig).astype(
            jnp.bfloat16
        )
        poly = jnp.full_like(small, log1p_terms[-1])
        for term in log1p_terms[-2::-1]:
            poly = poly * small + term
        loss = jnp.where(positive, size, 0.0) + small * poly
        part = jnp.sum(loss.reshape(TILE // 8, 8, N), axis=0)
        loss_sum = part if loss_sum is None else loss_sum + part
        text_grads.append(dot(pose_ref[...], weights_ref[cols(step), :], NT))
    loss_ref[...] = loss_sum

    pose_grads = [dot(text_ref[...], weights_ref[:, cols(0)], NN)]
    for step in range(STEPS):
        if step + 1 < STEPS:
            pose_grads.append(dot(text_ref[...], weights_ref[:, cols(step + 1)], NN))
        text_back_ref[:, :, :, cols(step)] = split(
            back_cols(text_grads[step], text_unit_ref[:, cols(step)], text_inverses[step])
        )
        store_halves(text_back_ref, 0, cols(step))
    for step in range(STEPS):
        back = back_cols(pose_grads[step], pose_unit_ref[:, cols(step)], pose_inverses[step])
        pose_back_ref[:, cols(step)] = back
    for step in range(STEPS):
        pose_term_ref[:, :, :, cols(step)] = split(
            dot(pose_back_ref[...], pose_feats_ref[:, cols(step)], NN)
        )
        store_halves(pose_term_ref, 1, cols(step))
        pose_rows_ref[cols(step), :] = pose_back_ref[:, cols(step)].T
        store(pose_rows_ref.at[cols(step), :], pose_rows_hbm.at[cols(step), :])
    for copy in out:
        copy.wait()


def loss_block(value):
    high = value.astype(jnp.bfloat16)
    rest = value - high.astype(jnp.float32)
    middle = rest.astype(jnp.bfloat16)
    low = (rest - middle.astype(jnp.float32)).astype(jnp.bfloat16)
    rows = lax.broadcasted_iota(jnp.int32, (16, 2 * ROWS), 0)
    block = jnp.where(
        rows == 0,
        high.astype(jnp.float32),
        jnp.where(
            rows == 1,
            middle.astype(jnp.float32),
            jnp.where(rows == 2, low.astype(jnp.float32), 0.0),
        ),
    )
    return block.astype(jnp.bfloat16)


def sum_loss(blocks):
    sums = jnp.sum(blocks.astype(jnp.float32), axis=0)
    return jnp.sum(sums[:3], axis=0, keepdims=True)


def terms_kernel(both_ref, own_ref, other_ref, loss_ref, out_ref):
    second = lax.axis_index("core")

    def text_cols(half):
        return both_ref[:ROWS, pl.ds(pl.multiple_of(half * (N // 2), N // 2), N // 2)]

    text_term = dot(text_cols(second), own_ref[...], NN)
    text_term += dot(text_cols(1 - second), other_ref[...], NN)
    text_term = text_term.astype(jnp.bfloat16)
    block = loss_block(jnp.full((16, 2 * ROWS), jnp.sum(loss_ref[...]), jnp.float32))
    for place in range(8):
        where = slice(place * 2 * ROWS, (place + 1) * 2 * ROWS)
        for high in range(2):
            out_ref[place * 2 + high, :ROWS, :] = both_ref[ROWS:, where]
            out_ref[place * 2 + high, ROWS : 2 * ROWS, :] = text_term[:, where]
            out_ref[place * 2 + high, 2 * ROWS :, :] = block


def turn_kernel(plane_ref, rows_ref, out_ref):
    sums = jnp.sum(plane_ref[:, : 2 * ROWS, :].astype(jnp.float32), axis=0).T.astype(jnp.bfloat16)
    total = sum_loss(plane_ref[:, 2 * ROWS :, :])
    block = loss_block(jnp.broadcast_to(total, (16, 2 * ROWS)))
    for core in range(NC):
        for z in range(NZ):
            out_ref[core * NZ + z, :ROWS, :] = sums[core * ROWS : (core + 1) * ROWS]
            out_ref[core * NZ + z, ROWS : ROWS + 32, :] = rows_ref[core * NZ + z]
            out_ref[core * NZ + z, ROWS + 32 :, :] = block


def last_kernel(line_ref, head_ref, grad_ref, heads_ref, loss_ref, text_ref):
    for m in range(16):
        text_ref[m * ROWS : m * ROWS + 32, :] = line_ref[m, ROWS : ROWS + 32, :ROWS]
        text_ref[m * ROWS + 32 : (m + 1) * ROWS, :] = line_ref[m, ROWS : ROWS + 32, ROWS:]
    grad_ref[...] = dot(text_ref[...], head_ref[...], TT)
    for m in range(0, 16, 2):
        for kind in range(2):
            lanes = slice(kind * ROWS, (kind + 1) * ROWS)
            pair = [line_ref[m + i, :ROWS, lanes].astype(jnp.float32) for i in range(2)]
            heads_ref[:, kind * N + m * ROWS : kind * N + (m + 2) * ROWS] = jnp.concatenate(
                pair, axis=1
            )
    total = sum_loss(line_ref[:, ROWS + 32 :, :]) / float(N * 16) ** 2
    loss_ref[...] = total[:, :1]


VMEM = pl.BlockSpec(memory_space=pltpu.VMEM)
ANY = pl.BlockSpec(memory_space=pl.ANY)


def shape(rows, dtype):
    return jax.ShapeDtypeStruct((rows, N), dtype)


def score(scale, grad_scale, pose_pieces, pose_head, text_own, text_other, text_head):
    half = pltpu.VMEM((N, N), jnp.bfloat16)
    full = pltpu.VMEM((N, N), jnp.float32)
    blocks = pltpu.VMEM((2, 8, ROWS, N), jnp.bfloat16)
    return pl.pallas_call(
        functools.partial(pair_kernel, scale, grad_scale),
        out_shape=(
            shape(8, jnp.float32),
            shape(N, jnp.bfloat16),
            jax.ShapeDtypeStruct((8, 2, ROWS, N), jnp.bfloat16),
            jax.ShapeDtypeStruct((8, 2, ROWS, N), jnp.bfloat16),
        ),
        in_specs=[ANY] * 9,
        out_specs=(VMEM, ANY, ANY, ANY),
        scratch_shapes=[
            pltpu.VMEM((N, N + EXTRA), jnp.bfloat16),
            half,
            half,
            half,
            half,
            full,
            half,
            full,
            half,
            blocks,
            half,
            half,
            blocks,
            pltpu.SemaphoreType.DMA((20,)),
            pltpu.SemaphoreType.DMA(((4 * NZ + 1) * STEPS,)),
        ],
        compiler_params=pltpu.CompilerParams(vmem_limit_bytes=58 * 1024 * 1024),
        cost_estimate=pl.CostEstimate(
            flops=12 * N**3, bytes_accessed=20 * N * N, transcendentals=2 * N * N
        ),
    )(*pose_pieces, pose_head, text_own, text_other, text_head)


def small_call(kernel, out_shape, scratch, *args):
    return pl.pallas_call(
        kernel,
        out_shape=out_shape,
        in_specs=[VMEM] * len(args),
        out_specs=jax.tree.map(lambda _: VMEM, out_shape),
        scratch_shapes=scratch,
        compiler_params=pltpu.CompilerParams(vmem_limit_bytes=16 * 1024 * 1024),
        cost_estimate=pl.CostEstimate(
            flops=2 * ROWS * N * N, bytes_accessed=4 * N * N, transcendentals=0
        ),
    )(*args)


def fold(blocks):
    return jnp.concatenate([blocks[:, : ROWS // 2], blocks[:, ROWS // 2 :]], axis=2)


def along_z(by):
    return lambda x, y, z, c: (x, y, z + by, c)


def ring_sum(keep, got):
    half = keep.shape[1] // 2

    def own(by):
        return keep[by % NZ].astype(jnp.float32) + got[by % NZ].astype(jnp.float32)

    def bf(value):
        return value.astype(jnp.bfloat16)

    up = send(bf(own(4)[:half]), along_z(1))
    down = send(bf(own(4)[half:]), along_z(-1))
    for by in (3, 2, 1):
        upper, lower = own(by), own(-by)
        if by == 3:
            up = jnp.concatenate([upper[:half] + up.astype(jnp.float32), upper[half:]])
            down = jnp.concatenate([lower[:half], lower[half:] + down.astype(jnp.float32)])
        else:
            up = upper + up.astype(jnp.float32)
            down = lower + down.astype(jnp.float32)
        up = send(bf(up), along_z(1))
        down = send(bf(down), along_z(-1))
    return bf(own(0) + up.astype(jnp.float32) + down.astype(jnp.float32))


def repeat_kernel(rows_hbm, out_hbm, sems):
    copies = [pltpu.make_async_copy(rows_hbm, out_hbm.at[b], sems.at[b]) for b in range(NZ)]
    for copy in copies:
        copy.start()
    for copy in copies:
        copy.wait()


def repeat(rows):
    return pl.pallas_call(
        repeat_kernel,
        out_shape=jax.ShapeDtypeStruct((NZ, *rows.shape), rows.dtype),
        in_specs=[ANY],
        out_specs=ANY,
        scratch_shapes=[pltpu.SemaphoreType.DMA((NZ,))],
        compiler_params=pltpu.CompilerParams(vmem_limit_bytes=1024 * 1024),
    )(rows)


def local(pose_feats, text_feats, match, pose_head, text_head):
    batch_size = ROWS * 256
    logit_scale = 2.0 * math.sqrt(N)
    grad_scale = logit_scale / math.sqrt(batch_size)
    x = lax.axis_index("x")
    y = lax.axis_index("yh") * 2 + lax.axis_index("yl")
    first = lax.axis_index("core") == 0

    text_own = lax.all_to_all(repeat(text_feats), "z", 0, 0)
    text_own = text_own.reshape(NZ * ROWS, N)
    ids = jnp.stack([match // 128, match % 128], axis=1).astype(jnp.bfloat16)
    shard = jnp.concatenate([pose_feats, jnp.pad(ids, ((0, 0), (0, EXTRA - 2)))], axis=1)
    column = jnp.zeros((4 * ROWS, N + EXTRA), jnp.bfloat16)
    for value, offset, start in ring_pieces(shard, plane_move(1)):
        place = jnp.where(first, y_slot((y + offset) % 4), (x + offset) % 4)
        column = lax.dynamic_update_slice(column, value, (place * ROWS + start, 0))
    pieces = [piece for piece, _, _ in ring_pieces(column, plane_move(0))]
    text_own, *pieces[3:] = lax.optimization_barrier((text_own, *pieces[3:]))
    text_other = swap_cores(text_own)

    loss_part, pose_part, keep, give = score(
        logit_scale, grad_scale, pieces, pose_head, text_own, text_other, text_head
    )
    got = swap_cores(give)
    pose_parts = lax.all_to_all(pose_part.reshape(16, ROWS, N), PLANE, 0, 0)
    both = ring_sum(keep.reshape(NZ, 2 * ROWS, N), got.reshape(NZ, 2 * ROWS, N))

    both, pose_parts = lax.optimization_barrier((both, pose_parts))
    pose_back = jnp.sum(pose_parts.astype(jnp.float32), axis=0).astype(jnp.bfloat16)
    grad_pose = dot(pose_back, pose_head, NT)

    bf16 = jnp.bfloat16
    terms = small_call(
        terms_kernel,
        jax.ShapeDtypeStruct((16, 2 * ROWS + 16, 2 * ROWS), bf16),
        [],
        both,
        text_own,
        text_other,
        loss_part,
    )
    plane = lax.all_to_all(terms, PLANE, 0, 0)
    text_rows = fold(both[:ROWS].reshape(ROWS, 16, ROWS).transpose(1, 0, 2))
    turned = small_call(
        turn_kernel,
        jax.ShapeDtypeStruct((16, ROWS + 48, 2 * ROWS), bf16),
        [],
        plane,
        text_rows,
    )
    line = lax.all_to_all(turned, LINE, 0, 0)
    grad_text, head_grads, loss = small_call(
        last_kernel,
        (
            shape(ROWS, jnp.float32),
            jax.ShapeDtypeStruct((ROWS, 2 * N), jnp.float32),
            jax.ShapeDtypeStruct((1, 1), jnp.float32),
        ),
        [pltpu.VMEM((N, ROWS), bf16)],
        line,
        text_head,
    )
    return (loss.reshape(()), grad_pose, grad_text, head_grads)


def solution(mesh):
    fine = Mesh(mesh.devices.reshape(NX, 2, NC, 2, NZ), AXES)
    placed = (P(AXES, None), P(AXES, None), P(AXES), P(), P())
    return jax.shard_map(
        local,
        mesh=fine,
        in_specs=placed,
        out_specs=(P(), P(AXES, None), P(AXES, None), P(("x", "yl", "core"), None)),
        check_vma=False,
    )
```

```python
import functools
import math

import jax
import jax.numpy as jnp
from jax import lax
from jax.experimental import pallas as pl
from jax.experimental.pallas import tpu as pltpu
from jax.sharding import Mesh
from jax.sharding import PartitionSpec as P

epsilon = 1e-06
logit_bias = -10.0
log1p_terms = (
    0.9999997615814209,
    -0.49997174739837646,
    0.3327192962169647,
    -0.24474774301052094,
    0.1768747717142105,
    -0.1068500280380249,
    0.04349390044808388,
    -0.00837115291506052,
)

AXES = ("x", "yl", "core", "yh", "z")
PLANE = ("x", "yl", "yh")
LINE = ("core", "z")
NX, NY, NZ, NC = 4, 4, 8, 2
ROWS = 64
N = 1024
EXTRA = 128
TILE = 512
STEPS = N // TILE

NT = (((1,), (1,)), ((), ()))
TN = (((0,), (0,)), ((), ()))
NN = (((1,), (0,)), ((), ()))
TT = (((0,), (1,)), ((), ()))


def device_index(x, y, z, c):
    return (((x * 2 + y % 2) * 2 + c) * 2 + y // 2) * NZ + z


def pairs_of(move):
    out = []
    for x in range(NX):
        for y in range(NY):
            for z in range(NZ):
                for c in range(NC):
                    x2, y2, z2, c2 = move(x, y, z, c)
                    out.append(
                        (device_index(x, y, z, c), device_index(x2 % NX, y2 % NY, z2 % NZ, c2 % NC))
                    )
    return out


def send(value, move):
    return lax.ppermute(value, AXES, pairs_of(move))


def swap_cores(value):
    return send(value, lambda x, y, z, c: (x, y, z, 1 - c))


def ring_pieces(shard, move):
    half = shard.shape[0] // 2
    below = send(shard, move(1))
    above = send(shard, move(-1))
    far_low = send(below[:half], move(1))
    far_high = send(above[half:], move(-1))
    return ((shard, 0, 0), (below, 3, 0), (above, 1, 0), (far_low, 2, 0), (far_high, 2, half))


def plane_move(x_core):
    def move_by(by):
        def move(x, y, z, c):
            return (x + by, y, z, c) if c == x_core else (x, y + by, z, c)

        return move

    return move_by


def y_slot(y):
    return y % 2 * 2 + y // 2


def dot(a, b, dims):
    return lax.dot_general(a, b, dims, preferred_element_type=jnp.float32)


def inverse_norm(raw):
    return lax.rsqrt(jnp.sum(raw * raw, axis=0, keepdims=True) + epsilon)


def reciprocal(value):
    guess = pltpu.reciprocal(value, approx=True)
    return guess * (2.0 - value * guess)


def back_cols(grad, unit, inverse):
    inner = jnp.sum(unit * grad, axis=0, keepdims=True)
    return ((grad - unit * inner) * inverse).astype(jnp.bfloat16)


def cols(step):
    return slice(step * TILE, (step + 1) * TILE)


def pair_kernel(
    scale,
    grad_scale,
    near_hbm,
    below_hbm,
    above_hbm,
    far_low_hbm,
    far_high_hbm,
    pose_head_hbm,
    text_own_hbm,
    text_other_hbm,
    text_head_hbm,
    loss_ref,
    pose_rows_hbm,
    keep_hbm,
    give_hbm,
    keep_far_hbm,
    give_far_hbm,
    pose_feats_ref,
    pose_head_ref,
    text_feats_ref,
    text_head_ref,
    pose_ref,
    pose_unit_ref,
    text_ref,
    text_unit_ref,
    weights_ref,
    text_back_ref,
    pose_back_ref,
    pose_rows_ref,
    pose_term_ref,
    in_sems,
    out_sems,
):
    second = lax.axis_index("core")
    out = []

    def fetch(source, target, number):
        copy = pltpu.make_async_copy(source, target, in_sems.at[number])
        copy.start()
        return copy

    def store(source, target):
        copy = pltpu.make_async_copy(source, target, out_sems.at[len(out)])
        copy.start()
        out.append(copy)

    def store_halves(source, kind, where):
        for half, target in (
            (second, (keep_hbm, keep_far_hbm)),
            (1 - second, (give_hbm, give_far_hbm)),
        ):
            for by in range(NZ):
                block = lax.rem(lax.axis_index("z") + by, NZ)
                if by == NZ // 2:
                    to = target[1].at[kind, :, where]
                else:
                    to = target[0].at[by - by // (NZ // 2 + 1), kind, :, where]
                store(source.at[half, block, :, where], to)

    def split(value):
        return value.astype(jnp.bfloat16).reshape(2, 8, ROWS, value.shape[1])

    def half_rows(half):
        return pl.ds(pl.multiple_of(half * (N // 2), N // 2), N // 2)

    pose_head_in = fetch(pose_head_hbm, pose_head_ref, 0)
    pose_in = []
    x, y = lax.axis_index("x"), lax.axis_index("yh") * 2 + lax.axis_index("yl")
    for source, offset, first in (
        (near_hbm, 0, 0),
        (below_hbm, 3, 0),
        (above_hbm, 1, 0),
        (far_low_hbm, 2, 0),
        (far_high_hbm, 2, 2),
    ):
        x_at = lax.rem(x + offset, 4)
        y_at = lax.rem(y + offset, 4)
        y_at = lax.rem(y_at, 2) * 2 + y_at // 2
        for block in range(source.shape[0] // ROWS):
            place = jnp.where(second == 0, x_at * 4 + first + block, (first + block) * 4 + y_at)
            at = pl.multiple_of(place * ROWS, ROWS)
            pose_in.append(
                fetch(
                    source.at[block * ROWS : (block + 1) * ROWS, :],
                    pose_feats_ref.at[pl.ds(at, ROWS), :],
                    1 + len(pose_in),
                )
            )
    text_head_in = fetch(text_head_hbm, text_head_ref, 17)
    own_in = fetch(text_own_hbm, text_feats_ref.at[half_rows(second), :], 18)
    other_in = fetch(text_other_hbm, text_feats_ref.at[half_rows(1 - second), :], 19)

    pose_raws, text_raws = [], []
    pose_head_in.wait()
    for copy in pose_in:
        copy.wait()
    for step in range(STEPS):
        pose_raws.append(dot(pose_head_ref[...], pose_feats_ref[cols(step), :N], TT))
    text_head_in.wait()
    own_in.wait()
    other_in.wait()
    pose_inverses, text_inverses = [], []
    for step in range(STEPS):
        text_raws.append(dot(text_head_ref[...], text_feats_ref[cols(step), :], TT))
        pose_inverses.append(inverse_norm(pose_raws[step]))
        unit = pose_raws[step] * pose_inverses[step]
        pose_unit_ref[:, cols(step)] = unit
        pose_ref[:, cols(step)] = unit.astype(jnp.bfloat16)
    for step in range(STEPS):
        text_inverses.append(inverse_norm(text_raws[step]))
        unit = text_raws[step] * text_inverses[step]
        text_unit_ref[:, cols(step)] = unit
        text_ref[:, cols(step)] = unit.astype(jnp.bfloat16)

    lanes = lax.broadcasted_iota(jnp.int32, (8, EXTRA), 1)
    pick = jnp.where(lanes == 0, 128.0, jnp.where(lanes == 1, 1.0, 0.0)).astype(jnp.bfloat16)
    match = dot(pick, pose_feats_ref[:, N:], NT).astype(jnp.int32)[0:1, :]
    place = lax.axis_index("x") * 2 + lax.axis_index("yl")
    offset = match - (place * 2048 + lax.axis_index("yh") * 512)
    late = offset >= 1024
    within = jnp.where(late, offset - 1024, offset)
    inside = (within >= 0) & (within < 512)
    target = jnp.where(inside, within + jnp.where(late, 512, 0), -1)

    inner = [dot(text_ref[:, cols(0)], pose_ref[...], TN)]
    loss_sum = None
    text_grads = []
    for step in range(STEPS):
        if step + 1 < STEPS:
            inner.append(dot(text_ref[:, cols(step + 1)], pose_ref[...], TN))
        logits = scale * inner[step] + logit_bias
        ids = lax.broadcasted_iota(jnp.int32, (TILE, 1), 0) + step * TILE
        paired = ids == target
        positive = paired != (logits >= 0.0)
        size = jnp.abs(logits)
        small = jnp.exp(-size)
        sig = jnp.where(positive, 1.0, small) * reciprocal(1.0 + small)
        weights_ref[cols(step), :] = (jnp.where(paired, -grad_scale, grad_scale) * sig).astype(
            jnp.bfloat16
        )
        poly = jnp.full_like(small, log1p_terms[-1])
        for term in log1p_terms[-2::-1]:
            poly = poly * small + term
        loss = jnp.where(positive, size, 0.0) + small * poly
        part = jnp.sum(loss.reshape(TILE // 8, 8, N), axis=0)
        loss_sum = part if loss_sum is None else loss_sum + part
        text_grads.append(dot(pose_ref[...], weights_ref[cols(step), :], NT))
    loss_ref[...] = loss_sum

    pose_grads = [dot(text_ref[...], weights_ref[:, cols(0)], NN)]
    for step in range(STEPS):
        if step + 1 < STEPS:
            pose_grads.append(dot(text_ref[...], weights_ref[:, cols(step + 1)], NN))
        text_back_ref[:, :, :, cols(step)] = split(
            back_cols(text_grads[step], text_unit_ref[:, cols(step)], text_inverses[step])
        )
        store_halves(text_back_ref, 0, cols(step))
    for step in range(STEPS):
        back = back_cols(pose_grads[step], pose_unit_ref[:, cols(step)], pose_inverses[step])
        pose_back_ref[:, cols(step)] = back
    for step in range(STEPS):
        pose_term_ref[:, :, :, cols(step)] = split(
            dot(pose_back_ref[...], pose_feats_ref[:, cols(step)], NN)
        )
        store_halves(pose_term_ref, 1, cols(step))
        pose_rows_ref[cols(step), :] = pose_back_ref[:, cols(step)].T
        store(pose_rows_ref.at[cols(step), :], pose_rows_hbm.at[cols(step), :])
    for copy in out:
        copy.wait()


def loss_block(value):
    high = value.astype(jnp.bfloat16)
    rest = value - high.astype(jnp.float32)
    middle = rest.astype(jnp.bfloat16)
    low = (rest - middle.astype(jnp.float32)).astype(jnp.bfloat16)
    rows = lax.broadcasted_iota(jnp.int32, (16, 2 * ROWS), 0)
    block = jnp.where(
        rows == 0,
        high.astype(jnp.float32),
        jnp.where(
            rows == 1,
            middle.astype(jnp.float32),
            jnp.where(rows == 2, low.astype(jnp.float32), 0.0),
        ),
    )
    return block.astype(jnp.bfloat16)


def sum_loss(blocks):
    sums = jnp.sum(blocks.astype(jnp.float32), axis=0)
    return jnp.sum(sums[:3], axis=0, keepdims=True)


def terms_kernel(both_ref, own_ref, other_ref, loss_ref, out_ref):
    second = lax.axis_index("core")

    def text_cols(half):
        return both_ref[:ROWS, pl.ds(pl.multiple_of(half * (N // 2), N // 2), N // 2)]

    text_term = dot(text_cols(second), own_ref[...], NN)
    text_term += dot(text_cols(1 - second), other_ref[...], NN)
    text_term = text_term.astype(jnp.bfloat16)
    block = loss_block(jnp.full((16, 2 * ROWS), jnp.sum(loss_ref[...]), jnp.float32))
    for place in range(8):
        where = slice(place * 2 * ROWS, (place + 1) * 2 * ROWS)
        for high in range(2):
            out_ref[place * 2 + high, :ROWS, :] = both_ref[ROWS:, where]
            out_ref[place * 2 + high, ROWS : 2 * ROWS, :] = text_term[:, where]
            out_ref[place * 2 + high, 2 * ROWS :, :] = block


def turn_kernel(plane_ref, rows_ref, out_ref):
    sums = jnp.sum(plane_ref[:, : 2 * ROWS, :].astype(jnp.float32), axis=0).T.astype(jnp.bfloat16)
    total = sum_loss(plane_ref[:, 2 * ROWS :, :])
    block = loss_block(jnp.broadcast_to(total, (16, 2 * ROWS)))
    for core in range(NC):
        for z in range(NZ):
            out_ref[core * NZ + z, :ROWS, :] = sums[core * ROWS : (core + 1) * ROWS]
            out_ref[core * NZ + z, ROWS : ROWS + 32, :] = rows_ref[core * NZ + z]
            out_ref[core * NZ + z, ROWS + 32 :, :] = block


def last_kernel(line_ref, head_ref, grad_ref, heads_ref, loss_ref, text_ref):
    for m in range(16):
        text_ref[m * ROWS : m * ROWS + 32, :] = line_ref[m, ROWS : ROWS + 32, :ROWS]
        text_ref[m * ROWS + 32 : (m + 1) * ROWS, :] = line_ref[m, ROWS : ROWS + 32, ROWS:]
    grad_ref[...] = dot(text_ref[...], head_ref[...], TT)
    for m in range(0, 16, 2):
        for kind in range(2):
            lanes = slice(kind * ROWS, (kind + 1) * ROWS)
            pair = [line_ref[m + i, :ROWS, lanes].astype(jnp.float32) for i in range(2)]
            heads_ref[:, kind * N + m * ROWS : kind * N + (m + 2) * ROWS] = jnp.concatenate(
                pair, axis=1
            )
    total = sum_loss(line_ref[:, ROWS + 32 :, :]) / float(N * 16) ** 2
    loss_ref[...] = total[:, :1]


VMEM = pl.BlockSpec(memory_space=pltpu.VMEM)
ANY = pl.BlockSpec(memory_space=pl.ANY)


def shape(rows, dtype):
    return jax.ShapeDtypeStruct((rows, N), dtype)


def score(scale, grad_scale, pose_pieces, pose_head, text_own, text_other, text_head):
    half = pltpu.VMEM((N, N), jnp.bfloat16)
    full = pltpu.VMEM((N, N), jnp.float32)
    blocks = pltpu.VMEM((2, 8, ROWS, N), jnp.bfloat16)
    return pl.pallas_call(
        functools.partial(pair_kernel, scale, grad_scale),
        out_shape=(
            shape(8, jnp.float32),
            shape(N, jnp.bfloat16),
            jax.ShapeDtypeStruct((7, 2, ROWS, N), jnp.bfloat16),
            jax.ShapeDtypeStruct((7, 2, ROWS, N), jnp.bfloat16),
            jax.ShapeDtypeStruct((2, ROWS, N), jnp.bfloat16),
            jax.ShapeDtypeStruct((2, ROWS, N), jnp.bfloat16),
        ),
        in_specs=[ANY] * 9,
        out_specs=(VMEM,) + (ANY,) * 5,
        scratch_shapes=[
            pltpu.VMEM((N, N + EXTRA), jnp.bfloat16),
            half,
            half,
            half,
            half,
            full,
            half,
            full,
            half,
            blocks,
            half,
            half,
            blocks,
            pltpu.SemaphoreType.DMA((20,)),
            pltpu.SemaphoreType.DMA(((4 * NZ + 1) * STEPS,)),
        ],
        compiler_params=pltpu.CompilerParams(vmem_limit_bytes=58 * 1024 * 1024),
        cost_estimate=pl.CostEstimate(
            flops=12 * N**3, bytes_accessed=20 * N * N, transcendentals=2 * N * N
        ),
    )(*pose_pieces, pose_head, text_own, text_other, text_head)


def small_call(kernel, out_shape, scratch, *args):
    return pl.pallas_call(
        kernel,
        out_shape=out_shape,
        in_specs=[VMEM] * len(args),
        out_specs=jax.tree.map(lambda _: VMEM, out_shape),
        scratch_shapes=scratch,
        compiler_params=pltpu.CompilerParams(vmem_limit_bytes=16 * 1024 * 1024),
        cost_estimate=pl.CostEstimate(
            flops=2 * ROWS * N * N, bytes_accessed=4 * N * N, transcendentals=0
        ),
    )(*args)


def fold(blocks):
    return jnp.concatenate([blocks[:, : ROWS // 2], blocks[:, ROWS // 2 :]], axis=2)


def along_z(by):
    return lambda x, y, z, c: (x, y, z + by, c)


def ring_sum(keep, got, keep_far, got_far):
    half = keep.shape[1] // 2

    def own(by):
        at = by if by >= 0 else by + 7
        return keep[at].astype(jnp.float32) + got[at].astype(jnp.float32)

    def bf(value):
        return value.astype(jnp.bfloat16)

    up = send(bf(keep_far[0].astype(jnp.float32) + got_far[0].astype(jnp.float32)), along_z(1))
    down = send(bf(keep_far[1].astype(jnp.float32) + got_far[1].astype(jnp.float32)), along_z(-1))
    for by in (3, 2, 1):
        upper, lower = own(by), own(-by)
        if by == 3:
            up = jnp.concatenate([upper[:half] + up.astype(jnp.float32), upper[half:]])
            down = jnp.concatenate([lower[:half], lower[half:] + down.astype(jnp.float32)])
        else:
            up = upper + up.astype(jnp.float32)
            down = lower + down.astype(jnp.float32)
        up = send(bf(up), along_z(1))
        down = send(bf(down), along_z(-1))
    return bf(own(0) + up.astype(jnp.float32) + down.astype(jnp.float32))


def repeat_kernel(rows_hbm, out_hbm, sems):
    copies = [pltpu.make_async_copy(rows_hbm, out_hbm.at[b], sems.at[b]) for b in range(NZ)]
    for copy in copies:
        copy.start()
    for copy in copies:
        copy.wait()


def repeat(rows):
    return pl.pallas_call(
        repeat_kernel,
        out_shape=jax.ShapeDtypeStruct((NZ, *rows.shape), rows.dtype),
        in_specs=[ANY],
        out_specs=ANY,
        scratch_shapes=[pltpu.SemaphoreType.DMA((NZ,))],
        compiler_params=pltpu.CompilerParams(vmem_limit_bytes=1024 * 1024),
    )(rows)


def local(pose_feats, text_feats, match, pose_head, text_head):
    batch_size = ROWS * 256
    logit_scale = 2.0 * math.sqrt(N)
    grad_scale = logit_scale / math.sqrt(batch_size)
    x = lax.axis_index("x")
    y = lax.axis_index("yh") * 2 + lax.axis_index("yl")
    first = lax.axis_index("core") == 0

    text_own = lax.all_to_all(repeat(text_feats), "z", 0, 0)
    text_own = text_own.reshape(NZ * ROWS, N)
    ids = jnp.stack([match // 128, match % 128], axis=1).astype(jnp.bfloat16)
    shard = jnp.concatenate([pose_feats, jnp.pad(ids, ((0, 0), (0, EXTRA - 2)))], axis=1)
    column = jnp.zeros((4 * ROWS, N + EXTRA), jnp.bfloat16)
    for value, offset, start in ring_pieces(shard, plane_move(1)):
        place = jnp.where(first, y_slot((y + offset) % 4), (x + offset) % 4)
        column = lax.dynamic_update_slice(column, value, (place * ROWS + start, 0))
    pieces = [piece for piece, _, _ in ring_pieces(column, plane_move(0))]
    text_own, *pieces[3:] = lax.optimization_barrier((text_own, *pieces[3:]))
    text_other = swap_cores(text_own)

    loss_part, pose_part, keep, give, keep_far, give_far = score(
        logit_scale, grad_scale, pieces, pose_head, text_own, text_other, text_head
    )
    got_far = swap_cores(give_far)
    got = swap_cores(give)
    pose_parts = lax.all_to_all(pose_part.reshape(16, ROWS, N), PLANE, 0, 0)
    both = ring_sum(
        keep.reshape(7, 2 * ROWS, N), got.reshape(7, 2 * ROWS, N), keep_far, got_far
    )

    both, pose_parts = lax.optimization_barrier((both, pose_parts))
    pose_back = jnp.sum(pose_parts.astype(jnp.float32), axis=0).astype(jnp.bfloat16)
    grad_pose = dot(pose_back, pose_head, NT)

    bf16 = jnp.bfloat16
    terms = small_call(
        terms_kernel,
        jax.ShapeDtypeStruct((16, 2 * ROWS + 16, 2 * ROWS), bf16),
        [],
        both,
        text_own,
        text_other,
        loss_part,
    )
    plane = lax.all_to_all(terms, PLANE, 0, 0)
    text_rows = fold(both[:ROWS].reshape(ROWS, 16, ROWS).transpose(1, 0, 2))
    turned = small_call(
        turn_kernel,
        jax.ShapeDtypeStruct((16, ROWS + 48, 2 * ROWS), bf16),
        [],
        plane,
        text_rows,
    )
    line = lax.all_to_all(turned, LINE, 0, 0)
    grad_text, head_grads, loss = small_call(
        last_kernel,
        (
            shape(ROWS, jnp.float32),
            jax.ShapeDtypeStruct((ROWS, 2 * N), jnp.float32),
            jax.ShapeDtypeStruct((1, 1), jnp.float32),
        ),
        [pltpu.VMEM((N, ROWS), bf16)],
        line,
        text_head,
    )
    return (loss.reshape(()), grad_pose, grad_text, head_grads)


def solution(mesh):
    fine = Mesh(mesh.devices.reshape(NX, 2, NC, 2, NZ), AXES)
    placed = (P(AXES, None), P(AXES, None), P(AXES), P(), P())
    return jax.shard_map(
        local,
        mesh=fine,
        in_specs=placed,
        out_specs=(P(), P(AXES, None), P(AXES, None), P(("x", "yl", "core"), None)),
        check_vma=False,
    )
```

```python
import functools
import math

import jax
import jax.numpy as jnp
from jax import lax
from jax.experimental import pallas as pl
from jax.experimental.pallas import tpu as pltpu
from jax.sharding import Mesh
from jax.sharding import PartitionSpec as P

epsilon = 1e-06
logit_bias = -10.0
log1p_terms = (
    0.9999997615814209,
    -0.49997174739837646,
    0.3327192962169647,
    -0.24474774301052094,
    0.1768747717142105,
    -0.1068500280380249,
    0.04349390044808388,
    -0.00837115291506052,
)

AXES = ("x", "yl", "core", "yh", "z")
PLANE = ("x", "yl", "yh")
LINE = ("core", "z")
NX, NY, NZ, NC = 4, 4, 8, 2
ROWS = 64
N = 1024
EXTRA = 128
TILE = 512
STEPS = N // TILE

NT = (((1,), (1,)), ((), ()))
TN = (((0,), (0,)), ((), ()))
NN = (((1,), (0,)), ((), ()))
TT = (((0,), (1,)), ((), ()))


def device_index(x, y, z, c):
    return (((x * 2 + y % 2) * 2 + c) * 2 + y // 2) * NZ + z


def pairs_of(move):
    out = []
    for x in range(NX):
        for y in range(NY):
            for z in range(NZ):
                for c in range(NC):
                    x2, y2, z2, c2 = move(x, y, z, c)
                    out.append(
                        (device_index(x, y, z, c), device_index(x2 % NX, y2 % NY, z2 % NZ, c2 % NC))
                    )
    return out


def send(value, move):
    return lax.ppermute(value, AXES, pairs_of(move))


def swap_cores(value):
    return send(value, lambda x, y, z, c: (x, y, z, 1 - c))


def ring_pieces(shard, move):
    half = shard.shape[0] // 2
    below = send(shard, move(1))
    above = send(shard, move(-1))
    far_low = send(below[:half], move(1))
    far_high = send(above[half:], move(-1))
    return ((shard, 0, 0), (below, 3, 0), (above, 1, 0), (far_low, 2, 0), (far_high, 2, half))


def plane_move(x_core):
    def move_by(by):
        def move(x, y, z, c):
            return (x + by, y, z, c) if c == x_core else (x, y + by, z, c)

        return move

    return move_by


def y_slot(y):
    return y % 2 * 2 + y // 2


def dot(a, b, dims):
    return lax.dot_general(a, b, dims, preferred_element_type=jnp.float32)


def inverse_norm(raw):
    return lax.rsqrt(jnp.sum(raw * raw, axis=0, keepdims=True) + epsilon)


def reciprocal(value):
    guess = pltpu.reciprocal(value, approx=True)
    return guess * (2.0 - value * guess)


def back_cols(grad, unit, inverse):
    inner = jnp.sum(unit * grad, axis=0, keepdims=True)
    return ((grad - unit * inner) * inverse).astype(jnp.bfloat16)


def cols(step):
    return slice(step * TILE, (step + 1) * TILE)


def pair_kernel(
    scale,
    grad_scale,
    near_hbm,
    below_hbm,
    above_hbm,
    far_low_hbm,
    far_high_hbm,
    pose_head_hbm,
    text_own_hbm,
    text_other_hbm,
    text_head_hbm,
    loss_ref,
    pose_rows_hbm,
    keep_hbm,
    give_hbm,
    keep_far_hbm,
    give_far_hbm,
    pose_feats_ref,
    pose_head_ref,
    text_feats_ref,
    text_head_ref,
    pose_ref,
    pose_unit_ref,
    text_ref,
    text_unit_ref,
    weights_ref,
    text_back_ref,
    pose_back_ref,
    pose_rows_ref,
    pose_term_ref,
    in_sems,
    out_sems,
):
    second = lax.axis_index("core")
    out = []

    def fetch(source, target, number):
        copy = pltpu.make_async_copy(source, target, in_sems.at[number])
        copy.start()
        return copy

    def store(source, target):
        copy = pltpu.make_async_copy(source, target, out_sems.at[len(out)])
        copy.start()
        out.append(copy)

    def store_halves(source, kind, where):
        for half, target in (
            (second, (keep_hbm, keep_far_hbm)),
            (1 - second, (give_hbm, give_far_hbm)),
        ):
            for by in range(NZ):
                block = lax.rem(lax.axis_index("z") + by, NZ)
                if by == NZ // 2:
                    to = target[1].at[kind, :, where]
                else:
                    to = target[0].at[by - by // (NZ // 2 + 1), kind, :, where]
                store(source.at[half, block, :, where], to)

    def split(value):
        return value.astype(jnp.bfloat16).reshape(2, 8, ROWS, value.shape[1])

    def half_rows(half):
        return pl.ds(pl.multiple_of(half * (N // 2), N // 2), N // 2)

    pose_head_in = fetch(pose_head_hbm, pose_head_ref, 0)
    pose_in = []
    x, y = lax.axis_index("x"), lax.axis_index("yh") * 2 + lax.axis_index("yl")
    for source, offset, first in (
        (near_hbm, 0, 0),
        (below_hbm, 3, 0),
        (above_hbm, 1, 0),
        (far_low_hbm, 2, 0),
        (far_high_hbm, 2, 2),
    ):
        x_at = lax.rem(x + offset, 4)
        y_at = lax.rem(y + offset, 4)
        y_at = lax.rem(y_at, 2) * 2 + y_at // 2
        for block in range(source.shape[0] // ROWS):
            place = jnp.where(second == 0, x_at * 4 + first + block, (first + block) * 4 + y_at)
            at = pl.multiple_of(place * ROWS, ROWS)
            pose_in.append(
                fetch(
                    source.at[block * ROWS : (block + 1) * ROWS, :],
                    pose_feats_ref.at[pl.ds(at, ROWS), :],
                    1 + len(pose_in),
                )
            )

    pose_raws, text_raws = [], []
    pose_head_in.wait()
    for copy in pose_in:
        copy.wait()
    text_head_in = fetch(text_head_hbm, text_head_ref, 17)
    own_in = fetch(text_own_hbm, text_feats_ref.at[half_rows(second), :], 18)
    other_in = fetch(text_other_hbm, text_feats_ref.at[half_rows(1 - second), :], 19)
    for step in range(STEPS):
        pose_raws.append(dot(pose_head_ref[...], pose_feats_ref[cols(step), :N], TT))
    text_head_in.wait()
    own_in.wait()
    other_in.wait()
    pose_inverses, text_inverses = [], []
    for step in range(STEPS):
        text_raws.append(dot(text_head_ref[...], text_feats_ref[cols(step), :], TT))
        pose_inverses.append(inverse_norm(pose_raws[step]))
        unit = pose_raws[step] * pose_inverses[step]
        pose_unit_ref[:, cols(step)] = unit
        pose_ref[:, cols(step)] = unit.astype(jnp.bfloat16)
    for step in range(STEPS):
        text_inverses.append(inverse_norm(text_raws[step]))
        unit = text_raws[step] * text_inverses[step]
        text_unit_ref[:, cols(step)] = unit
        text_ref[:, cols(step)] = unit.astype(jnp.bfloat16)

    lanes = lax.broadcasted_iota(jnp.int32, (8, EXTRA), 1)
    pick = jnp.where(lanes == 0, 128.0, jnp.where(lanes == 1, 1.0, 0.0)).astype(jnp.bfloat16)
    match = dot(pick, pose_feats_ref[:, N:], NT).astype(jnp.int32)[0:1, :]
    place = lax.axis_index("x") * 2 + lax.axis_index("yl")
    offset = match - (place * 2048 + lax.axis_index("yh") * 512)
    late = offset >= 1024
    within = jnp.where(late, offset - 1024, offset)
    inside = (within >= 0) & (within < 512)
    target = jnp.where(inside, within + jnp.where(late, 512, 0), -1)

    inner = [dot(text_ref[:, cols(0)], pose_ref[...], TN)]
    loss_sum = None
    text_grads = []
    for step in range(STEPS):
        if step + 1 < STEPS:
            inner.append(dot(text_ref[:, cols(step + 1)], pose_ref[...], TN))
        logits = scale * inner[step] + logit_bias
        ids = lax.broadcasted_iota(jnp.int32, (TILE, 1), 0) + step * TILE
        paired = ids == target
        positive = paired != (logits >= 0.0)
        size = jnp.abs(logits)
        small = jnp.exp(-size)
        sig = jnp.where(positive, 1.0, small) * reciprocal(1.0 + small)
        weights_ref[cols(step), :] = (jnp.where(paired, -grad_scale, grad_scale) * sig).astype(
            jnp.bfloat16
        )
        poly = jnp.full_like(small, log1p_terms[-1])
        for term in log1p_terms[-2::-1]:
            poly = poly * small + term
        loss = jnp.where(positive, size, 0.0) + small * poly
        part = jnp.sum(loss.reshape(TILE // 8, 8, N), axis=0)
        loss_sum = part if loss_sum is None else loss_sum + part
        text_grads.append(dot(pose_ref[...], weights_ref[cols(step), :], NT))
    loss_ref[...] = loss_sum

    pose_grads = [dot(text_ref[...], weights_ref[:, cols(0)], NN)]
    for step in range(STEPS):
        if step + 1 < STEPS:
            pose_grads.append(dot(text_ref[...], weights_ref[:, cols(step + 1)], NN))
        text_back_ref[:, :, :, cols(step)] = split(
            back_cols(text_grads[step], text_unit_ref[:, cols(step)], text_inverses[step])
        )
        store_halves(text_back_ref, 0, cols(step))
    for step in range(STEPS):
        back = back_cols(pose_grads[step], pose_unit_ref[:, cols(step)], pose_inverses[step])
        pose_back_ref[:, cols(step)] = back
        pose_rows_ref[cols(step), :] = pose_back_ref[:, cols(step)].T
        store(pose_rows_ref.at[cols(step), :], pose_rows_hbm.at[cols(step), :])
    for step in range(STEPS):
        pose_term_ref[:, :, :, cols(step)] = split(
            dot(pose_back_ref[...], pose_feats_ref[:, cols(step)], NN)
        )
        store_halves(pose_term_ref, 1, cols(step))
    for copy in out:
        copy.wait()


def loss_block(value):
    high = value.astype(jnp.bfloat16)
    rest = value - high.astype(jnp.float32)
    middle = rest.astype(jnp.bfloat16)
    low = (rest - middle.astype(jnp.float32)).astype(jnp.bfloat16)
    rows = lax.broadcasted_iota(jnp.int32, (16, 2 * ROWS), 0)
    block = jnp.where(
        rows == 0,
        high.astype(jnp.float32),
        jnp.where(
            rows == 1,
            middle.astype(jnp.float32),
            jnp.where(rows == 2, low.astype(jnp.float32), 0.0),
        ),
    )
    return block.astype(jnp.bfloat16)


def sum_loss(blocks):
    sums = jnp.sum(blocks.astype(jnp.float32), axis=0)
    return jnp.sum(sums[:3], axis=0, keepdims=True)


def terms_kernel(both_ref, own_ref, other_ref, loss_ref, out_ref):
    second = lax.axis_index("core")

    def text_cols(half):
        return both_ref[:ROWS, pl.ds(pl.multiple_of(half * (N // 2), N // 2), N // 2)]

    text_term = dot(text_cols(second), own_ref[...], NN)
    text_term += dot(text_cols(1 - second), other_ref[...], NN)
    text_term = text_term.astype(jnp.bfloat16)
    block = loss_block(jnp.full((16, 2 * ROWS), jnp.sum(loss_ref[...]), jnp.float32))
    for place in range(8):
        where = slice(place * 2 * ROWS, (place + 1) * 2 * ROWS)
        for high in range(2):
            out_ref[place * 2 + high, :ROWS, :] = both_ref[ROWS:, where]
            out_ref[place * 2 + high, ROWS : 2 * ROWS, :] = text_term[:, where]
            out_ref[place * 2 + high, 2 * ROWS :, :] = block


def turn_kernel(plane_ref, rows_ref, out_ref):
    sums = jnp.sum(plane_ref[:, : 2 * ROWS, :].astype(jnp.float32), axis=0).T.astype(jnp.bfloat16)
    total = sum_loss(plane_ref[:, 2 * ROWS :, :])
    block = loss_block(jnp.broadcast_to(total, (16, 2 * ROWS)))
    for core in range(NC):
        for z in range(NZ):
            out_ref[core * NZ + z, :ROWS, :] = sums[core * ROWS : (core + 1) * ROWS]
            out_ref[core * NZ + z, ROWS : ROWS + 32, :] = rows_ref[core * NZ + z]
            out_ref[core * NZ + z, ROWS + 32 :, :] = block


def last_kernel(line_ref, head_ref, grad_ref, heads_ref, loss_ref, text_ref):
    for m in range(16):
        text_ref[m * ROWS : m * ROWS + 32, :] = line_ref[m, ROWS : ROWS + 32, :ROWS]
        text_ref[m * ROWS + 32 : (m + 1) * ROWS, :] = line_ref[m, ROWS : ROWS + 32, ROWS:]
    grad_ref[...] = dot(text_ref[...], head_ref[...], TT)
    for m in range(0, 16, 2):
        for kind in range(2):
            lanes = slice(kind * ROWS, (kind + 1) * ROWS)
            pair = [line_ref[m + i, :ROWS, lanes].astype(jnp.float32) for i in range(2)]
            heads_ref[:, kind * N + m * ROWS : kind * N + (m + 2) * ROWS] = jnp.concatenate(
                pair, axis=1
            )
    total = sum_loss(line_ref[:, ROWS + 32 :, :]) / float(N * 16) ** 2
    loss_ref[...] = total[:, :1]


VMEM = pl.BlockSpec(memory_space=pltpu.VMEM)
ANY = pl.BlockSpec(memory_space=pl.ANY)


def shape(rows, dtype):
    return jax.ShapeDtypeStruct((rows, N), dtype)


def score(scale, grad_scale, pose_pieces, pose_head, text_own, text_other, text_head):
    half = pltpu.VMEM((N, N), jnp.bfloat16)
    full = pltpu.VMEM((N, N), jnp.float32)
    blocks = pltpu.VMEM((2, 8, ROWS, N), jnp.bfloat16)
    return pl.pallas_call(
        functools.partial(pair_kernel, scale, grad_scale),
        out_shape=(
            shape(8, jnp.float32),
            shape(N, jnp.bfloat16),
            jax.ShapeDtypeStruct((7, 2, ROWS, N), jnp.bfloat16),
            jax.ShapeDtypeStruct((7, 2, ROWS, N), jnp.bfloat16),
            jax.ShapeDtypeStruct((2, ROWS, N), jnp.bfloat16),
            jax.ShapeDtypeStruct((2, ROWS, N), jnp.bfloat16),
        ),
        in_specs=[ANY] * 9,
        out_specs=(VMEM,) + (ANY,) * 5,
        scratch_shapes=[
            pltpu.VMEM((N, N + EXTRA), jnp.bfloat16),
            half,
            half,
            half,
            half,
            full,
            half,
            full,
            half,
            blocks,
            half,
            half,
            blocks,
            pltpu.SemaphoreType.DMA((20,)),
            pltpu.SemaphoreType.DMA(((4 * NZ + 1) * STEPS,)),
        ],
        compiler_params=pltpu.CompilerParams(vmem_limit_bytes=58 * 1024 * 1024),
        cost_estimate=pl.CostEstimate(
            flops=12 * N**3, bytes_accessed=20 * N * N, transcendentals=2 * N * N
        ),
    )(*pose_pieces, pose_head, text_own, text_other, text_head)


def small_call(kernel, out_shape, scratch, *args):
    return pl.pallas_call(
        kernel,
        out_shape=out_shape,
        in_specs=[VMEM] * len(args),
        out_specs=jax.tree.map(lambda _: VMEM, out_shape),
        scratch_shapes=scratch,
        compiler_params=pltpu.CompilerParams(vmem_limit_bytes=16 * 1024 * 1024),
        cost_estimate=pl.CostEstimate(
            flops=2 * ROWS * N * N, bytes_accessed=4 * N * N, transcendentals=0
        ),
    )(*args)


def fold(blocks):
    return jnp.concatenate([blocks[:, : ROWS // 2], blocks[:, ROWS // 2 :]], axis=2)


def along_z(by):
    return lambda x, y, z, c: (x, y, z + by, c)


def ring_sum(keep, got, keep_far, got_far):
    half = keep.shape[1] // 2

    def own(by):
        at = by if by >= 0 else by + 7
        return keep[at].astype(jnp.float32) + got[at].astype(jnp.float32)

    def bf(value):
        return value.astype(jnp.bfloat16)

    up = send(bf(keep_far[0].astype(jnp.float32) + got_far[0].astype(jnp.float32)), along_z(1))
    down = send(bf(keep_far[1].astype(jnp.float32) + got_far[1].astype(jnp.float32)), along_z(-1))
    for by in (3, 2, 1):
        upper, lower = own(by), own(-by)
        if by == 3:
            up = jnp.concatenate([upper[:half] + up.astype(jnp.float32), upper[half:]])
            down = jnp.concatenate([lower[:half], lower[half:] + down.astype(jnp.float32)])
        else:
            up = upper + up.astype(jnp.float32)
            down = lower + down.astype(jnp.float32)
        up = send(bf(up), along_z(1))
        down = send(bf(down), along_z(-1))
    return bf(own(0) + up.astype(jnp.float32) + down.astype(jnp.float32))


def repeat_kernel(rows_hbm, out_hbm, sems):
    copies = [pltpu.make_async_copy(rows_hbm, out_hbm.at[b], sems.at[b]) for b in range(NZ)]
    for copy in copies:
        copy.start()
    for copy in copies:
        copy.wait()


def repeat(rows):
    return pl.pallas_call(
        repeat_kernel,
        out_shape=jax.ShapeDtypeStruct((NZ, *rows.shape), rows.dtype),
        in_specs=[ANY],
        out_specs=ANY,
        scratch_shapes=[pltpu.SemaphoreType.DMA((NZ,))],
        compiler_params=pltpu.CompilerParams(vmem_limit_bytes=1024 * 1024),
    )(rows)


def local(pose_feats, text_feats, match, pose_head, text_head):
    batch_size = ROWS * 256
    logit_scale = 2.0 * math.sqrt(N)
    grad_scale = logit_scale / math.sqrt(batch_size)
    x = lax.axis_index("x")
    y = lax.axis_index("yh") * 2 + lax.axis_index("yl")
    first = lax.axis_index("core") == 0

    text_own = lax.all_to_all(repeat(text_feats), "z", 0, 0)
    text_own = text_own.reshape(NZ * ROWS, N)
    ids = jnp.stack([match // 128, match % 128], axis=1).astype(jnp.bfloat16)
    shard = jnp.concatenate([pose_feats, jnp.pad(ids, ((0, 0), (0, EXTRA - 2)))], axis=1)
    column = jnp.zeros((4 * ROWS, N + EXTRA), jnp.bfloat16)
    for value, offset, start in ring_pieces(shard, plane_move(1)):
        place = jnp.where(first, y_slot((y + offset) % 4), (x + offset) % 4)
        column = lax.dynamic_update_slice(column, value, (place * ROWS + start, 0))
    pieces = [piece for piece, _, _ in ring_pieces(column, plane_move(0))]
    text_own, *pieces[3:] = lax.optimization_barrier((text_own, *pieces[3:]))
    text_other = swap_cores(text_own)

    loss_part, pose_part, keep, give, keep_far, give_far = score(
        logit_scale, grad_scale, pieces, pose_head, text_own, text_other, text_head
    )
    got_far = swap_cores(give_far)
    got = swap_cores(give)
    pose_parts = lax.all_to_all(pose_part.reshape(16, ROWS, N), PLANE, 0, 0)
    both = ring_sum(
        keep.reshape(7, 2 * ROWS, N), got.reshape(7, 2 * ROWS, N), keep_far, got_far
    )

    both, pose_parts = lax.optimization_barrier((both, pose_parts))
    pose_back = jnp.sum(pose_parts.astype(jnp.float32), axis=0).astype(jnp.bfloat16)
    grad_pose = dot(pose_back, pose_head, NT)

    bf16 = jnp.bfloat16
    terms = small_call(
        terms_kernel,
        jax.ShapeDtypeStruct((16, 2 * ROWS + 16, 2 * ROWS), bf16),
        [],
        both,
        text_own,
        text_other,
        loss_part,
    )
    plane = lax.all_to_all(terms, PLANE, 0, 0)
    text_rows = fold(both[:ROWS].reshape(ROWS, 16, ROWS).transpose(1, 0, 2))
    turned = small_call(
        turn_kernel,
        jax.ShapeDtypeStruct((16, ROWS + 48, 2 * ROWS), bf16),
        [],
        plane,
        text_rows,
    )
    line = lax.all_to_all(turned, LINE, 0, 0)
    grad_text, head_grads, loss = small_call(
        last_kernel,
        (
            shape(ROWS, jnp.float32),
            jax.ShapeDtypeStruct((ROWS, 2 * N), jnp.float32),
            jax.ShapeDtypeStruct((1, 1), jnp.float32),
        ),
        [pltpu.VMEM((N, ROWS), bf16)],
        line,
        text_head,
    )
    return (loss.reshape(()), grad_pose, grad_text, head_grads)


def solution(mesh):
    fine = Mesh(mesh.devices.reshape(NX, 2, NC, 2, NZ), AXES)
    placed = (P(AXES, None), P(AXES, None), P(AXES), P(), P())
    return jax.shard_map(
        local,
        mesh=fine,
        in_specs=placed,
        out_specs=(P(), P(AXES, None), P(AXES, None), P(("x", "yl", "core"), None)),
        check_vma=False,
    )
```
